512 devices in a mesh: head: 4 (over x), vocab: 128 (over y, z, core).
Axes of the slice: x: 4, y: 4, z: 16, core: 2. Of those that a mesh axis runs over, the one named last changes fastest.
Arguments:
- hidden: bfloat16 [128, 4096], P(None, 'vocab'), may hold values from -6 to 6
- res_weight: bfloat16 [4, 4096, 4096], P('head', None, 'vocab'), may hold values from -0.09375 to 0.09375
- res_bias: float32 [4, 4096], P('head', 'vocab'), may hold values from -3 to 3
- out_weight: bfloat16 [4, 65536, 4096], P('head', 'vocab'), may hold values from -4 to 4
- targets: int32 [4, 128], P('head'), may hold values from 0 to 65535
- loss_mask: int32 [4, 128], P('head'), may hold values 0 or 1
Outputs:
- grad_hidden: float32 [128, 4096], P(None, 'vocab')
- grad_res_weight: float32 [4, 4096, 4096], P('head', None, 'vocab')
- grad_res_bias: float32 [4, 4096], P('head', 'vocab')
- head_loss: float32 [4], P('head')
The draws below stay inside these ranges and needn't reach their ends.
All inputs are finite; a program needn't handle non-finite values. No bound on the sum of `loss_mask` on one device may be relied on, other than what follows from the above.
Results may differ from the reference program's by a relative error of at most 0.0075.
The reference program's roundings to bfloat16 on the way count: a program that leaves them out, or rounds other values in their place, can miss the bound.
Values may be sent and summed in bfloat16 or wider, within the bound.
A program may use at most 64 MiB of HBM per device.

```python
import math
import jax
import jax.numpy as jnp
from jax import lax

D = 4096
ROWS = 128
HEADS = 4
V = 65536


def draw_out_weight(key, part):
    key = jax.random.fold_in(key, 11)
    first = jax.random.fold_in(key, 0)
    values = jax.random.normal(first, (HEADS, V, D), jnp.float32) * (3.0 / math.sqrt(D))
    return jnp.clip(values, -4.0, 4.0).astype(jnp.bfloat16)


def place_ends(array, own_key, smallest, high):
    spot = [jax.random.randint(jax.random.fold_in(own_key, axis), (), 0, length) for axis, length in enumerate(array.shape)]
    widest = array.shape.index(max(array.shape))
    beside = spot[:widest] + [(spot[widest] + 1) % array.shape[widest]] + spot[widest + 1:]
    return array.at[tuple(spot)].set(smallest).at[tuple(beside)].set(high)


def steps_of(rng, extent, pieces, low, high):
    level, own = 1.0, jax.random.fold_in(rng, 6)
    for dim, shards_of in pieces:
        draws = jnp.exp(jax.random.uniform(jax.random.fold_in(own, dim), (shards_of,), jnp.float32, low / len(pieces), high / len(pieces)))
        level = level * jnp.repeat(draws, extent[dim] // shards_of).reshape([-1 if axis == dim else 1 for axis in range(len(extent))])
    return level


def bell_draw(stream_key, dims, deviation, most, cuts=(), held_as=jnp.bfloat16):
    drawn = jax.random.normal(stream_key, dims, jnp.float32) * deviation
    if len(cuts) > 0:
        drawn = steps_of(stream_key, dims, cuts, -0.22, 0.18) * drawn
    return jnp.clip(drawn, min=-most, max=most).astype(held_as)


def setup_inputs(seed: int = 0) -> dict:
    key_list = jax.random.split(jax.random.key(seed), 7)
    return {
        "hidden": bell_draw(key_list[0], (ROWS, D), 1.0, 6.0, ((1, 128),)),
        "res_weight": bell_draw(key_list[1], (HEADS, D, D), D ** -0.5, 0.09375, ((0, 4), (2, 128))),
        "res_bias": bell_draw(key_list[2], (HEADS, D), 0.5, 3.0, ((0, 4), (1, 128)), jnp.float32),
        "out_weight": draw_out_weight(jax.random.fold_in(key_list[6], 71), 0),
        "targets": place_ends(jax.random.randint(key_list[4], (HEADS, ROWS), 0, V), jax.random.fold_in(key_list[4], 1), 0, V - 1).astype(jnp.int32),
        "loss_mask": place_ends((jax.random.randint(key_list[5], (HEADS, ROWS), 0, 4) < 3).astype(jnp.int32), jax.random.fold_in(key_list[5], 1), 0, 1),
    }


def reference(hidden, res_weight, res_bias, out_weight, targets, loss_mask):
    grad_input = jnp.zeros((ROWS, D), jnp.float32)
    weight_grads = []
    bias_grads = []
    losses = []
    vocab_ids = lax.broadcasted_iota(jnp.int32, (ROWS, V), 1)
    for head_id in range(HEADS):
        pre = jnp.dot(hidden, res_weight[head_id], preferred_element_type=jnp.float32) + res_bias[head_id][None, :]
        block_out = (hidden.astype(jnp.float32) + jax.nn.silu(pre)).astype(jnp.bfloat16)
        logits = lax.dot_general(block_out, out_weight[head_id], (((1,), (1,)), ((), ())), preferred_element_type=jnp.float32)
        top = jnp.max(logits, axis=1)
        total = jnp.sum(jnp.exp(logits - top[:, None]), axis=1)
        lse = top + jnp.log(total)
        onehot = vocab_ids == targets[head_id][:, None]
        picked = jnp.sum(jnp.where(onehot, logits, 0.0), axis=1)
        row_weight = (0.8 ** (head_id + 1)) * loss_mask[head_id].astype(jnp.float32) / ROWS
        losses.append(jnp.sum(row_weight * (lse - picked)))
        dlogits = (row_weight[:, None] * (jnp.exp(logits - lse[:, None]) - onehot.astype(jnp.float32))).astype(jnp.bfloat16)
        grad_block = jnp.dot(dlogits, out_weight[head_id], preferred_element_type=jnp.float32)
        sig = jax.nn.sigmoid(pre)
        dpre = (grad_block * sig * (1.0 + pre * (1.0 - sig))).astype(jnp.bfloat16)
        weight_grads.append(jnp.dot(hidden.T, dpre, preferred_element_type=jnp.float32))
        bias_grads.append(jnp.sum(dpre.astype(jnp.float32), axis=0))
        grad_input = grad_input + grad_block + jnp.dot(dpre, res_weight[head_id].T, preferred_element_type=jnp.float32)
    return grad_input, jnp.stack(weight_grads), jnp.stack(bias_grads), jnp.stack(losses)
```

```python
import functools

import jax
import jax.numpy as jnp
from jax import lax
from jax.experimental import pallas as pl
from jax.experimental.pallas import tpu as pltpu
from jax.sharding import PartitionSpec as P

MESH = pl.DeviceIdType.MESH
F32, BF16 = jnp.float32, jnp.bfloat16
GRID = {128: (4, 16), 16: (2, 4), 8: (2, 2)}
FEAT = 32
PARTS = 4


class Place:
    def __init__(self, heads, vocab):
        self.heads = heads
        self.ny, self.nz = GRID[vocab]
        v = lax.axis_index("vocab")
        self.x = lax.axis_index("head")
        self.v = v
        self.y = lax.div(v, 2 * self.nz)
        self.z = lax.rem(lax.div(v, 2), self.nz)
        self.c = lax.rem(v, 2)
        half = self.nz // 2
        self.dist = sorted(range(self.nz), key=lambda d: (-min(d, self.nz - d), d))
        self.slot_of = {d: j for j, d in enumerate(self.dist)}
        self.half = half
        self.parts = min(PARTS, self.nz)
        self.gs = self.nz // self.parts
        self.ydist = sorted(range(1, self.ny), key=lambda d: (-min(d, self.ny - d), d))

    def slot(self, z_abs):
        d = lax.rem(z_abs - self.z + self.nz, self.nz)
        return jnp.where(d >= self.half, jnp.where(d == self.half, 0, 2 * (d - self.half)), 2 * (self.half - d) - 1)

    def yat(self, d):
        return lax.rem(self.y + d + self.ny, self.ny)

    def zat(self, d):
        return lax.rem(self.z + d + self.nz, self.nz)

    def dev(self, y, z, c):
        return (self.x, (y * self.nz + z) * 2 + c)


def remote(src, dst, send, recv, dev):
    return pltpu.make_async_remote_copy(
        src_ref=src, dst_ref=dst, send_sem=send, recv_sem=recv, device_id=dev, device_id_type=MESH
    )


def gather(pt, buf, sems, sent):
    zs, zr, ys, yr, cs, cr = sems
    own = pt.nz - 1
    sib = pt.dev(pt.y, pt.z, 1 - pt.c)
    arrive_z = {}
    for j, d in enumerate(pt.dist[:-1]):
        there = pt.slot_of[(pt.nz - d) % pt.nz]
        cp = remote(
            buf.at[pt.c, pt.y, own], buf.at[pt.c, pt.y, there], zs.at[j], zr.at[there], pt.dev(pt.y, pt.zat(d), pt.c)
        )
        cp.start()
        sent.append(cp)
        arrive_z[there] = cp

    def group(core, y, g):
        return buf.at[core, y, pl.ds(g * pt.gs, pt.gs)]

    def across(p, y, g):
        cp = remote(group(pt.c, y, g), group(pt.c, y, g), cs.at[p, g], cr.at[p, g], sib)
        cp.start()
        sent.append(cp)

    def pass_on(g):
        for d in reversed(pt.ydist):
            y = pt.yat(-d)
            remote(group(pt.c, y, g), group(pt.c, y, g), ys.at[d - 1, g], yr.at[d - 1, g], sib).wait_recv()
            across(d, y, g)

    for g in reversed(range(pt.parts)):
        for j in range(g * pt.gs, (g + 1) * pt.gs):
            if j != own:
                arrive_z[j].wait_recv()
        for d in pt.ydist:
            cp = remote(
                group(pt.c, pt.y, g),
                group(pt.c, pt.y, g),
                ys.at[d - 1, g],
                yr.at[d - 1, g],
                pt.dev(pt.yat(d), pt.z, pt.c),
            )
            cp.start()
            sent.append(cp)
        across(0, pt.y, g)
        if g + 1 < pt.parts:
            pass_on(g + 1)
    pass_on(0)
    for g in reversed(range(pt.parts)):
        for p in range(pt.ny):
            y = pt.yat(-p)
            remote(group(1 - pt.c, y, g), group(1 - pt.c, y, g), cs.at[p, g], cr.at[p, g], sib).wait_recv()


def in_order(pt, buf, flat):
    def step(i, carry):
        y, z = lax.div(i, pt.nz), lax.rem(i, pt.nz)
        j = pt.slot(z)
        for core in range(2):
            flat[pl.ds(pl.multiple_of((i * 2 + core) * FEAT, FEAT), FEAT), :] = buf[core, y, j]
        return carry

    lax.fori_loop(0, pt.ny * pt.nz, step, 0, unroll=4)


def scatter(pt, theirs, mine, bufs, sems, sent, between=None):
    to_core, from_core, to_y, from_y, to_z, from_z = bufs
    cs, cr, ys, yr, zs, zr = sems
    sib = pt.dev(pt.y, pt.z, 1 - pt.c)
    n = pt.gs * FEAT
    last = pt.parts - 1

    def rows(g):
        return pl.ds(g * n, n)

    order = pt.ydist + [0]
    core_copies = {}
    for d in order:
        y = pt.yat(d)
        for g in range(pt.parts):
            to_core[d, rows(g), :] = theirs(y, g).astype(BF16)
        cp = remote(to_core.at[d], from_core.at[d], cs.at[d], cr.at[d], sib)
        cp.start()
        sent.append(cp)
        core_copies[d] = cp
    y_copies = {}
    for g in range(pt.parts):
        for d in pt.ydist:
            y = pt.yat(d)
            if g == 0:
                core_copies[d].wait_recv()
            to_y[d - 1, rows(g), :] = (mine(y, g) + from_core[d, rows(g), :].astype(F32)).astype(BF16)
            cp = remote(
                to_y.at[d - 1, rows(g)],
                from_y.at[d - 1, rows(g)],
                ys.at[d - 1, g],
                yr.at[d - 1, g],
                pt.dev(y, pt.z, pt.c),
            )
            cp.start()
            sent.append(cp)
            y_copies[d, g] = cp
    core_copies[0].wait_recv()
    if between is not None:
        between()
    total = None
    z_copies = []
    for g in range(pt.parts):
        acc = mine(pt.y, g) + from_core[0, rows(g), :].astype(F32)
        for d in reversed(pt.ydist):
            y_copies[d, g].wait_recv()
            acc = acc + from_y[d - 1, rows(g), :].astype(F32)
        to_z[rows(g), :] = acc.astype(BF16)
        if g == last:
            total = acc[n - FEAT :, :]
        for j in range(g * pt.gs, (g + 1) * pt.gs):
            if j == pt.nz - 1:
                continue
            d = pt.dist[j]
            there = pt.slot_of[(pt.nz - d) % pt.nz]
            cp = remote(
                to_z.at[pl.ds(j * FEAT, FEAT)],
                from_z.at[there],
                zs.at[j],
                zr.at[there],
                pt.dev(pt.y, pt.zat(d), pt.c),
            )
            cp.start()
            sent.append(cp)
            z_copies.append((there, cp))
    for there, cp in sorted(z_copies, key=lambda t: -t[0]):
        cp.wait_recv()
        total = total + from_z[there].astype(F32)
    return total


def kernel(heads, vocab, *refs):
    (hid, bias, tgt, msk, wres_hbm, wout_hbm, gh_out, gw_out, gb_out, loss_out) = refs[:10]
    (wo, wot, wr, wrt, buf1, buf2, flat1, flat2, logits, eo, prod, prod2, gw, st, st_y, sz, st_z, gx, gx_in) = refs[10:29]
    rs1, rs2 = refs[29:35], refs[35:41]
    ag1_s, ag2_s, rs1_s, rs2_s = refs[41:47], refs[47:53], refs[53:59], refs[59:65]
    sys_, syr, szs, szr, xs, xr, local = refs[65:72]
    pt = Place(heads, vocab)
    ny, nz = pt.ny, pt.nz
    nrow = hid.shape[1]
    nvoc = wo.shape[0]
    feats = wo.shape[1]
    ychunk = feats // ny
    sent = []

    get_wr = pltpu.make_async_copy(wres_hbm, wr, local.at[0])
    get_wo = pltpu.make_async_copy(wout_hbm, wo, local.at[1])
    get_wr.start()
    get_wo.start()

    peers = [pt.dev(pt.y, pt.zat(d), pt.c) for d in pt.dist[:-1]]
    plane = [(dy, dc) for dy in range(ny) for dc in range(2) if dy or dc]
    near = [pt.dev(pt.yat(dy), pt.z, lax.rem(pt.c + dc, 2)) for dy, dc in plane]
    xpeers = [(lax.rem(pt.x + d, heads), pt.v) for d in range(1, heads)]
    barrier = pltpu.get_barrier_semaphore()
    for dev in peers + near + xpeers:
        pl.semaphore_signal(barrier, inc=1, device_id=dev, device_id_type=MESH)
    buf1[pt.c, pt.y, nz - 1] = hid[...]

    per = 256 // (2 * FEAT)

    def place_rows(dst, chunk, i):
        y = lax.div(i * per, nz)
        z0 = lax.rem(i * per, nz)
        for k in range(per):
            j = pt.slot(z0 + k)
            for core in range(2):
                r = (k * 2 + core) * FEAT
                dst[core, y, j] = chunk[r : r + FEAT, :]

    def turn_wr(i, carry):
        place_rows(wrt, wr[:, pl.ds(pl.multiple_of(i * 256, 256), 256)].T, i)
        return carry

    get_wr.wait()
    lax.fori_loop(0, feats // 256, turn_wr, 0)
    pl.semaphore_wait(barrier, len(peers) + len(near) + len(xpeers))

    def turn_wo(i, carry):
        place_rows(wot, wo[:, pl.ds(pl.multiple_of(i * 256, 256), 256)].T, i)
        return carry

    gather(pt, buf1, ag1_s, sent)
    in_order(pt, buf1, flat1)

    eye = lax.broadcasted_iota(jnp.int32, (FEAT, FEAT), 0) == lax.broadcasted_iota(jnp.int32, (FEAT, FEAT), 1)
    bias_col = jnp.sum(jnp.where(eye, bias[...], 0.0), axis=1, keepdims=True)
    pre = jnp.zeros((FEAT, nrow), F32)
    for y in range(ny):
        pre = pre + jnp.dot(
            wr[:, y * ychunk : (y + 1) * ychunk], flat1[y * ychunk : (y + 1) * ychunk, :], preferred_element_type=F32
        )
    pre = pre + bias_col
    sig = jax.nn.sigmoid(pre)
    buf2[pt.c, pt.y, nz - 1] = (hid[...].astype(F32) + pre * sig).astype(BF16)
    gate = sig * (1.0 + pre * (1.0 - sig))

    get_wo.wait()
    lax.fori_loop(0, feats // 256, turn_wo, 0)
    gather(pt, buf2, ag2_s, sent)
    in_order(pt, buf2, flat2)

    logits[...] = jnp.zeros_like(logits)

    def logit_step(i, carry):
        at = pl.ds(pl.multiple_of(i * ychunk, ychunk), ychunk)
        logits[...] += jnp.dot(wo[:, at], flat2[at, :], preferred_element_type=F32)
        return carry

    lax.fori_loop(0, ny, logit_step, 0)
    ids = pt.v * nvoc + lax.broadcasted_iota(jnp.int32, (nvoc, nrow), 0)
    hit = ids == tgt[...]
    lg = logits[...]
    top = jnp.max(lg, axis=0, keepdims=True)
    picked = jnp.sum(jnp.where(hit, lg, 0.0), axis=0, keepdims=True)
    owned = jnp.sum(hit.astype(F32), axis=0, keepdims=True)
    e = jnp.exp(lg - top)
    tot = jnp.sum(e, axis=0, keepdims=True)
    eo[:, :nrow] = jnp.where(hit, 0.0, e).astype(BF16)
    eo[:, nrow:] = hit.astype(BF16)

    def pack(a, b, c):
        r = lax.broadcasted_iota(jnp.int32, (8, nrow), 0)
        return jnp.where(r == 0, a, jnp.where(r == 1, b, jnp.where(r == 2, c, 0.0)))

    def merge(ref, count):
        tops = [ref[i, 0:1, :] for i in range(count)]
        best = functools.reduce(jnp.maximum, tops)
        total = sum(ref[i, 1:2, :] * jnp.exp(tops[i] - best) for i in range(count))
        pick = sum(ref[i, 2:3, :] for i in range(count))
        return best, total, pick

    mine = pack(top, tot, picked)
    st[...] = mine
    me = pt.y * 2 + pt.c
    st_y[me] = mine
    y_copies = []
    for k, dev in enumerate(near):
        cp = remote(st, st_y.at[me], sys_.at[k], syr.at[k], dev)
        cp.start()
        sent.append(cp)
        y_copies.append(cp)

    def product(i, carry):
        core, y = lax.div(i, ny), lax.rem(i, ny)
        prod[core, y] = jnp.dot(
            wot[core, y].reshape(nz * FEAT, nvoc), eo[...], preferred_element_type=F32
        )
        return carry

    lax.fori_loop(0, ny, product, 0)
    for cp in y_copies:
        cp.wait_recv()
    mine = pack(*merge(st_y, ny * 2))
    sz[...] = mine
    st_z[pt.z] = mine
    z_copies = []
    for j, d in enumerate(pt.dist[:-1]):
        cp = remote(sz, st_z.at[pt.z], szs.at[j], szr.at[j], pt.dev(pt.y, pt.zat(d), pt.c))
        cp.start()
        sent.append(cp)
        z_copies.append(cp)
    lax.fori_loop(ny, 2 * ny, product, 0)
    for cp in z_copies:
        cp.wait_recv()
    best, total, pick = merge(st_z, nz)
    lse = best + jnp.log(total)
    factor = jnp.float32(0.8 ** heads)
    for k in range(heads - 1):
        factor = jnp.where(pt.x == k, jnp.float32(0.8 ** (k + 1)), factor)
    weight = factor * msk[...].astype(F32) / nrow
    loss_out[...] = jnp.sum(weight * (lse - pick), axis=1, keepdims=True)
    alpha = weight * jnp.exp(top - lse)
    beta = jnp.where(owned > 0.0, weight * (jnp.exp(picked - lse) - 1.0), 0.0).astype(BF16).astype(F32)

    n = pt.gs * FEAT

    def term(core, y, g):
        return alpha * prod[core, y, g * n : (g + 1) * n, :nrow] + beta * prod[core, y, g * n : (g + 1) * n, nrow:]

    dh = scatter(
        pt, lambda y, g: term(1 - pt.c, y, g), lambda y, g: term(pt.c, y, g), rs1, rs1_s, sent
    )
    dpre = (dh * gate).astype(BF16)
    gb = jnp.sum(dpre.astype(F32), axis=1, keepdims=True)
    gb_out[...] = jnp.sum(jnp.where(eye, gb, 0.0), axis=0, keepdims=True)

    for core in range(2):
        for y in range(ny):
            prod2[core, y] = jnp.dot(
                wrt[core, y].reshape(nz * FEAT, FEAT), dpre, preferred_element_type=F32
            )
    put_gw = pltpu.make_async_copy(gw, gw_out, local.at[2])

    def weight_grad():
        def step(i, carry):
            at = pl.ds(pl.multiple_of(i * 256, 256), 256)
            gw[:, at] = lax.dot_general(
                dpre, flat1[at, :], (((1,), (1,)), ((), ())), preferred_element_type=F32
            )
            return carry

        lax.fori_loop(0, feats // 256, step, 0)
        put_gw.start()

    back = scatter(
        pt,
        lambda y, g: prod2[1 - pt.c, y, g * n : (g + 1) * n, :],
        lambda y, g: prod2[pt.c, y, g * n : (g + 1) * n, :],
        rs2,
        rs2_s,
        sent,
        weight_grad,
    )
    part = dh + back
    gx[...] = part
    gx_in[pt.x] = part
    x_copies = []
    for k, dev in enumerate(xpeers):
        cp = remote(gx, gx_in.at[pt.x], xs.at[k], xr.at[k], dev)
        cp.start()
        sent.append(cp)
        x_copies.append(cp)
    for cp in x_copies:
        cp.wait_recv()
    gh_out[...] = sum(gx_in[k] for k in range(heads))
    for cp in sent:
        cp.wait_send()
    put_gw.wait()


def body(heads, vocab, hidden, res_weight, res_bias, out_weight, targets, loss_mask):
    ny, nz = GRID[vocab]
    rows = hidden.shape[0]
    nvoc, feats = out_weight.shape[1:]
    parts = min(PARTS, nz)
    dma = pltpu.SemaphoreType.DMA
    vm = pltpu.VMEM
    gather_sems = [dma((nz,)), dma((nz,)), dma((ny, parts)), dma((ny, parts)), dma((ny, parts)), dma((ny, parts))]
    scatter_sems = [dma((ny,)), dma((ny,)), dma((ny, parts)), dma((ny, parts)), dma((nz,)), dma((nz,))]
    scatter_bufs = [
        vm((ny, nz * FEAT, rows), BF16),
        vm((ny, nz * FEAT, rows), BF16),
        vm((ny - 1, nz * FEAT, rows), BF16),
        vm((ny - 1, nz * FEAT, rows), BF16),
        vm((nz * FEAT, rows), BF16),
        vm((nz, FEAT, rows), BF16),
    ]
    in_vmem = pl.BlockSpec(memory_space=pltpu.VMEM)
    anywhere = pl.BlockSpec(memory_space=pl.ANY)
    gh, gw, gb, loss = pl.pallas_call(
        functools.partial(kernel, heads, vocab),
        out_shape=(
            jax.ShapeDtypeStruct((FEAT, rows), F32),
            jax.ShapeDtypeStruct((FEAT, feats), F32),
            jax.ShapeDtypeStruct((1, FEAT), F32),
            jax.ShapeDtypeStruct((1, 1), F32),
        ),
        in_specs=[in_vmem] * 4 + [anywhere] * 2,
        out_specs=(in_vmem, anywhere, in_vmem, in_vmem),
        scratch_shapes=[
            vm((nvoc, feats), BF16),
            vm((2, ny, nz, FEAT, nvoc), BF16),
            vm((FEAT, feats), BF16),
            vm((2, ny, nz, FEAT, FEAT), BF16),
            vm((2, ny, nz, FEAT, rows), BF16),
            vm((2, ny, nz, FEAT, rows), BF16),
            vm((feats, rows), BF16),
            vm((feats, rows), BF16),
            vm((nvoc, rows), F32),
            vm((nvoc, 2 * rows), BF16),
            vm((2, ny, nz * FEAT, 2 * rows), F32),
            vm((2, ny, nz * FEAT, rows), F32),
            vm((FEAT, feats), F32),
            vm((8, rows), F32),
            vm((2 * ny, 8, rows), F32),
            vm((8, rows), F32),
            vm((nz, 8, rows), F32),
            vm((FEAT, rows), F32),
            vm((heads, FEAT, rows), F32),
            *scatter_bufs,
            *scatter_bufs,
            *gather_sems,
            *gather_sems,
            *scatter_sems,
            *scatter_sems,
            dma((2 * ny,)),
            dma((2 * ny,)),
            dma((nz,)),
            dma((nz,)),
            dma((max(heads - 1, 1),)),
            dma((max(heads - 1, 1),)),
            dma((3,)),
        ],
        name="heads_backward",
        compiler_params=pltpu.CompilerParams(
            collective_id=0, has_side_effects=True, vmem_limit_bytes=48 << 20
        ),
    )(hidden.T, res_bias, targets, loss_mask, res_weight[0].T, out_weight[0])
    return gh.T, gw.T[None], gb, loss.reshape(1)


def solution(mesh):
    placed = (
        P(None, "vocab"),
        P("head", None, "vocab"),
        P("head", "vocab"),
        P("head", "vocab", None),
        P("head", None),
        P("head", None),
    )
    return jax.shard_map(
        functools.partial(body, mesh.shape["head"], mesh.shape["vocab"]),
        mesh=mesh,
        in_specs=placed,
        out_specs=(P(None, "vocab"), P("head", None, "vocab"), P("head", "vocab"), P("head")),
        check_vma=False,
    )
```

```python
import functools

import jax
import jax.numpy as jnp
from jax import lax
from jax.experimental import pallas as pl
from jax.experimental.pallas import tpu as pltpu
from jax.sharding import PartitionSpec as P

MESH = pl.DeviceIdType.MESH
F32, BF16 = jnp.float32, jnp.bfloat16
GRID = {128: (4, 16), 16: (2, 4), 8: (2, 2)}
FEAT = 32
PARTS = 4
NEAR = 8


class Place:
    def __init__(self, heads, vocab):
        self.heads = heads
        self.ny, self.nz = GRID[vocab]
        v = lax.axis_index("vocab")
        self.x = lax.axis_index("head")
        self.v = v
        self.y = lax.div(v, 2 * self.nz)
        self.z = lax.rem(lax.div(v, 2), self.nz)
        self.c = lax.rem(v, 2)
        half = self.nz // 2
        self.dist = sorted(range(self.nz), key=lambda d: (-min(d, self.nz - d), d))
        self.slot_of = {d: j for j, d in enumerate(self.dist)}
        self.half = half
        self.parts = min(PARTS, self.nz)
        self.gs = self.nz // self.parts
        self.near = min(NEAR, self.nz // 2)
        self.sib = (self.x, v + 1 - 2 * self.c)
        self.ydist = sorted(range(1, self.ny), key=lambda d: (-min(d, self.ny - d), d))

    def slot(self, z_abs):
        d = lax.rem(z_abs - self.z + self.nz, self.nz)
        return jnp.where(d >= self.half, jnp.where(d == self.half, 0, 2 * (d - self.half)), 2 * (self.half - d) - 1)

    def yat(self, d):
        return lax.rem(self.y + d + self.ny, self.ny)

    def zat(self, d):
        return lax.rem(self.z + d + self.nz, self.nz)

    def dev(self, y, z, c):
        return (self.x, (y * self.nz + z) * 2 + c)


def remote(src, dst, send, recv, dev):
    return pltpu.make_async_remote_copy(
        src_ref=src, dst_ref=dst, send_sem=send, recv_sem=recv, device_id=dev, device_id_type=MESH
    )


class Sends:
    def __init__(self, pt):
        self.pt = pt
        self.open = []

    def add(self, ref, sem):
        self.open.append((ref, sem))

    def flush(self):
        for ref, sem in self.open:
            remote(ref, ref, sem, sem, self.pt.sib).wait_send()
        self.open = []


def arrived(pt, ref, sem):
    remote(ref, ref, sem, sem, pt.sib).wait_recv()


def gather(pt, buf, sems, sends, between=None):
    zs, ys, cs, cr = (sems.at[k] for k in range(4))
    own = pt.nz - 1
    c = pt.c
    groups = ((pt.nz - pt.near, pt.nz), (0, pt.nz - pt.near))
    for d in pt.dist[:-1]:
        there = pt.slot_of[(pt.nz - d) % pt.nz]
        g = 0 if there >= groups[0][0] else 1
        remote(buf.at[c, 0, own], buf.at[c, 0, there], zs, sems.at[4 + g], pt.dev(pt.y, pt.zat(d), c)).start()
    if between is not None:
        between()

    def across(rows, lo, hi):
        part = buf.at[c, pl.ds(*rows), pl.ds(lo, hi - lo)]
        remote(part, part, cs, cr, pt.sib).start()

    for g, (lo, hi) in enumerate(groups):
        n = hi - lo - (g == 0)
        arrived(pt, buf.at[c, 0, pl.ds(lo, n)], sems.at[4 + g])
        for d in pt.ydist:
            remote(
                buf.at[c, 0, pl.ds(lo, hi - lo)],
                buf.at[c, d, pl.ds(lo, hi - lo)],
                ys,
                sems.at[6 + g],
                pt.dev(pt.yat(d), pt.z, c),
            ).start()
        across((0, 1), lo, hi)
    for g, (lo, hi) in enumerate(groups):
        arrived(pt, buf.at[c, pl.ds(1, pt.ny - 1), pl.ds(lo, hi - lo)], sems.at[6 + g])
        across((1, pt.ny - 1), lo, hi)
    arrived(pt, buf.at[1 - c], cr)
    sends.add(buf.at[c, 0, pl.ds(0, own)], zs)
    sends.add(buf.at[c, pl.ds(1, pt.ny - 1)], ys)
    sends.add(buf.at[c], cs)


def in_order(pt, buf, flat):
    def step(i, carry):
        y, z = lax.div(i, pt.nz), lax.rem(i, pt.nz)
        j = pt.slot(z)
        y = lax.rem(pt.y - y + pt.ny, pt.ny)
        for core in range(2):
            flat[pl.ds(pl.multiple_of((i * 2 + core) * FEAT, FEAT), FEAT), :] = buf[core, y, j]
        return carry

    lax.fori_loop(0, pt.ny * pt.nz, step, 0, unroll=4)


def scatter(pt, theirs, mine, bufs, sems, sends, beside=None, between=None, finish=None):
    to_core, from_core, to_y, from_y, to_z, from_z = bufs
    cs, ys, zs, zr = (sems.at[k] for k in range(4))
    n = pt.gs * FEAT
    last = pt.parts - 1

    def rows(g):
        return pl.ds(g * n, n)

    for d in pt.ydist + [0]:
        for g in range(pt.parts):
            to_core[d, rows(g), :] = theirs(pt.yat(d), g).astype(BF16)
        remote(to_core.at[d], from_core.at[d], cs, sems.at[4 + d], pt.sib).start()
    sends.flush()
    sends.add(to_core, cs)
    if beside is not None:
        beside()
    for g in range(pt.parts):
        for d in pt.ydist:
            if g == 0:
                arrived(pt, from_core.at[d], sems.at[4 + d])
            to_y[d - 1, rows(g), :] = (mine(pt.yat(d), g) + from_core[d, rows(g), :].astype(F32)).astype(BF16)
            remote(
                to_y.at[d - 1, rows(g)],
                from_y.at[d - 1, rows(g)],
                ys,
                sems.at[4 + pt.ny + g],
                pt.dev(pt.yat(d), pt.z, pt.c),
            ).start()
    sends.add(to_y, ys)
    arrived(pt, from_core.at[0], sems.at[4])
    if between is not None:
        between()
    for g in range(pt.parts):
        acc = mine(pt.y, g) + from_core[0, rows(g), :].astype(F32)
        arrived(pt, from_y.at[:, rows(g)], sems.at[4 + pt.ny + g])
        for d in pt.ydist:
            acc = acc + from_y[d - 1, rows(g), :].astype(F32)
        if finish is not None:
            acc = finish(acc, g)
        to_z[rows(g), :] = acc.astype(BF16)
        if g == last:
            total = acc[n - FEAT :, :]
        for j in range(g * pt.gs, (g + 1) * pt.gs):
            if j == pt.nz - 1:
                continue
            d = pt.dist[j]
            there = pt.slot_of[(pt.nz - d) % pt.nz]
            remote(
                to_z.at[pl.ds(j * FEAT, FEAT)], from_z.at[there], zs, zr, pt.dev(pt.y, pt.zat(d), pt.c)
            ).start()
    sends.flush()
    sends.add(to_z.at[pl.ds(0, (pt.nz - 1) * FEAT)], zs)
    arrived(pt, from_z.at[pl.ds(0, pt.nz - 1)], zr)
    for j in range(pt.nz - 1):
        total = total + from_z[j].astype(F32)
    return total


def kernel(heads, vocab, *refs):
    (hid_hbm, bias_hbm, tgt_hbm, msk_hbm, wres_hbm, wout_hbm, gh_out, gw_out, gb_out, loss_out) = refs[:10]
    (wo, wot, wr, wrt, buf1, buf2, flat1, flat2, logits, eo, prod, prod2, gw, st, st_y, sz, st_z, gx, gx_in) = refs[10:29]
    rs1, rs2 = refs[29:35], refs[35:41]
    t_to_core, t_from_core, t_mine, t_to_y, t_from_y = refs[41:46]
    ag1_s, ag2_s, rs1_s, rs2_s, t_s, tail_s, local = refs[46:53]
    bias, tgt, msk = refs[53:56]
    pt = Place(heads, vocab)
    ny, nz = pt.ny, pt.nz
    nrow = buf1.shape[-1]
    nvoc = wo.shape[0]
    feats = wo.shape[1]
    ychunk = feats // ny
    sends = Sends(pt)

    hid = buf1.at[pt.c, 0, nz - 1]
    get_wr = pltpu.make_async_copy(wres_hbm, wr, local.at[0])
    get_wo = pltpu.make_async_copy(wout_hbm, wo, local.at[1])
    get_hid = pltpu.make_async_copy(hid_hbm, hid, local.at[3])
    get_small = [
        pltpu.make_async_copy(src, dst, local.at[4 + k])
        for k, (src, dst) in enumerate(((bias_hbm, bias), (tgt_hbm, tgt), (msk_hbm, msk)))
    ]
    for cp in [get_hid, get_wr, *get_small, get_wo]:
        cp.start()

    peers = [pt.dev(pt.y, pt.zat(d), pt.c) for d in pt.dist[:-1]]
    plane = [(dy, dc) for dy in range(ny) for dc in range(2) if dy or dc]
    near = [pt.dev(pt.yat(dy), pt.z, lax.rem(pt.c + dc, 2)) for dy, dc in plane]
    xpeers = [(lax.rem(pt.x + d, heads), pt.v) for d in range(1, heads)]
    barrier = pltpu.get_barrier_semaphore()
    for dev in peers + near + xpeers:
        pl.semaphore_signal(barrier, inc=1, device_id=dev, device_id_type=MESH)

    per = 256 // (2 * FEAT)

    def place_rows(dst, chunk, i):
        y = lax.div(i * per, nz)
        z0 = lax.rem(i * per, nz)
        for k in range(per):
            j = pt.slot(z0 + k)
            for core in range(2):
                r = (k * 2 + core) * FEAT
                dst[core, y, j] = chunk[r : r + FEAT, :]

    def turn_wr(i, carry):
        place_rows(wrt, wr[:, pl.ds(pl.multiple_of(i * 256, 256), 256)].T, i)
        return carry

    for cp in get_small:
        cp.wait()
    get_hid.wait()
    pl.semaphore_wait(barrier, len(peers) + len(near) + len(xpeers))

    def turn_wo(i, carry):
        place_rows(wot, wo[:, pl.ds(pl.multiple_of(i * 256, 256), 256)].T, i)
        return carry

    def turn():
        get_wr.wait()
        lax.fori_loop(0, feats // 256, turn_wr, 0)
        get_wo.wait()
        lax.fori_loop(0, feats // 256, turn_wo, 0)

    gather(pt, buf1, ag1_s, sends, turn)
    in_order(pt, buf1, flat1)

    eye = lax.broadcasted_iota(jnp.int32, (FEAT, FEAT), 0) == lax.broadcasted_iota(jnp.int32, (FEAT, FEAT), 1)
    bias_col = jnp.sum(jnp.where(eye, bias[...], 0.0), axis=1, keepdims=True)
    pre = jnp.zeros((FEAT, nrow), F32)
    for y in range(ny):
        pre = pre + jnp.dot(
            wr[:, y * ychunk : (y + 1) * ychunk], flat1[y * ychunk : (y + 1) * ychunk, :], preferred_element_type=F32
        )
    pre = pre + bias_col
    sig = jax.nn.sigmoid(pre)
    buf2[pt.c, 0, nz - 1] = (hid[...].astype(F32) + pre * sig).astype(BF16)
    gate = sig * (1.0 + pre * (1.0 - sig))

    ids = pt.v * nvoc + lax.broadcasted_iota(jnp.int32, (nvoc, nrow), 0)
    hit = ids == tgt[...]

    def target_rows():
        sends.flush()
        eo[...] = hit.astype(BF16)

        def rows_of(core, y):
            w = wot[core, y].reshape(nz * FEAT, nvoc)
            return jnp.dot(w, eo[...], preferred_element_type=F32).astype(BF16)

        for d in range(ny):
            t_to_core[d] = rows_of(1 - pt.c, pt.yat(d))
        remote(t_to_core, t_from_core, t_s.at[0], t_s.at[1], pt.sib).start()
        for d in range(ny):
            t_mine[d] = rows_of(pt.c, pt.yat(d))
        arrived(pt, t_from_core, t_s.at[1])
        for d in pt.ydist:
            t_to_y[d - 1] = t_mine[d] + t_from_core[d]
            remote(t_to_y.at[d - 1], t_from_y.at[d - 1], t_s.at[2], t_s.at[3], pt.dev(pt.yat(d), pt.z, pt.c)).start()
        sends.add(t_to_core, t_s.at[0])
        sends.add(t_to_y, t_s.at[2])

    gather(pt, buf2, ag2_s, sends, target_rows)
    in_order(pt, buf2, flat2)

    logits[...] = jnp.zeros_like(logits)

    def logit_step(i, carry):
        at = pl.ds(pl.multiple_of(i * ychunk, ychunk), ychunk)
        logits[...] += jnp.dot(wo[:, at], flat2[at, :], preferred_element_type=F32)
        return carry

    lax.fori_loop(0, ny, logit_step, 0)
    lg = logits[...]
    top = jnp.max(lg, axis=0, keepdims=True)
    picked = jnp.sum(jnp.where(hit, lg, 0.0), axis=0, keepdims=True)
    e = jnp.exp(lg - top)
    e_hit = jnp.sum(jnp.where(hit, e, 0.0), axis=0, keepdims=True)
    e = jnp.where(hit, 0.0, e)
    rest = jnp.sum(e, axis=0, keepdims=True)
    eo[...] = e.astype(BF16)

    def pack(*values):
        r = lax.broadcasted_iota(jnp.int32, (8, nrow), 0)
        out = jnp.zeros((8, nrow), F32)
        for k, value in enumerate(values):
            out = jnp.where(r == k, value, out)
        return out

    def merge(ref, count):
        tops = [ref[i, 0:1, :] for i in range(count)]
        best = functools.reduce(jnp.maximum, tops)
        scale = [jnp.exp(t - best) for t in tops]
        others = sum(ref[i, 1:2, :] * scale[i] for i in range(count))
        target = sum(ref[i, 2:3, :] * scale[i] for i in range(count))
        pick = sum(ref[i, 3:4, :] for i in range(count))
        return best, others, target, pick

    packed = pack(top, rest, e_hit, picked)
    st[...] = packed
    me = pt.y * 2 + pt.c
    st_y[me] = packed
    for dev in near:
        remote(st, st_y.at[me], tail_s.at[0], tail_s.at[1], dev).start()

    def product(i, carry):
        core, y = lax.div(i, ny), lax.rem(i, ny)
        prod[core, y] = jnp.dot(wot[core, y].reshape(nz * FEAT, nvoc), eo[...], preferred_element_type=F32)
        return carry

    lax.fori_loop(0, 2 * ny, product, 0)
    arrived(pt, st_y.at[pl.ds(0, 2 * ny - 1)], tail_s.at[1])
    sends.add(st_y.at[pl.ds(0, 2 * ny - 1)], tail_s.at[0])
    plane_stats = merge(st_y, 2 * ny)
    plane_top = plane_stats[0]
    scale = jnp.exp(top - plane_top)
    n = pt.gs * FEAT

    def stats_out():
        packed = pack(*plane_stats)
        sz[...] = packed
        st_z[pt.z] = packed
        for d in pt.dist[:-1]:
            remote(sz, st_z.at[pt.z], tail_s.at[2], tail_s.at[3], pt.dev(pt.y, pt.zat(d), pt.c)).start()

    factors = []

    def stats_in():
        arrived(pt, st_z.at[pl.ds(0, nz - 1)], tail_s.at[3])
        sends.add(st_z.at[pl.ds(0, nz - 1)], tail_s.at[2])
        best, others, target, pick = merge(st_z, nz)
        total = others + target
        lse = best + jnp.log(total)
        factor = jnp.float32(0.8**heads)
        for k in range(heads - 1):
            factor = jnp.where(pt.x == k, jnp.float32(0.8 ** (k + 1)), factor)
        weight = factor * msk[...].astype(F32) / nrow
        loss_out[...] = jnp.sum(weight * (lse - pick), axis=1, keepdims=True)
        alpha = weight * jnp.exp(plane_top - lse)
        beta = (-weight * (others / total)).astype(BF16).astype(F32)
        factors.extend((alpha, beta))
        arrived(pt, t_from_y, t_s.at[3])

    def finish(acc, g):
        alpha, beta = factors
        at = pl.ds(g * n, n)
        rows = t_mine[0, at, :].astype(F32) + t_from_core[0, at, :].astype(F32)
        for d in pt.ydist:
            rows = rows + t_from_y[d - 1, at, :].astype(F32)
        return alpha * acc + beta * rows

    dh = scatter(
        pt,
        lambda y, g: scale * prod[1 - pt.c, y, g * n : (g + 1) * n, :],
        lambda y, g: scale * prod[pt.c, y, g * n : (g + 1) * n, :],
        rs1,
        rs1_s,
        sends,
        stats_out,
        stats_in,
        finish,
    )
    dpre = (dh * gate).astype(BF16)
    gb = jnp.sum(dpre.astype(F32), axis=1, keepdims=True)
    gb_out[...] = jnp.sum(jnp.where(eye, gb, 0.0), axis=0, keepdims=True)

    for core in range(2):
        for y in range(ny):
            prod2[core, y] = jnp.dot(
                wrt[core, y].reshape(nz * FEAT, FEAT), dpre, preferred_element_type=F32
            )
    put_gw = pltpu.make_async_copy(gw, gw_out, local.at[2])

    def weight_grad():
        def step(i, carry):
            at = pl.ds(pl.multiple_of(i * 256, 256), 256)
            gw[:, at] = lax.dot_general(
                dpre, flat1[at, :], (((1,), (1,)), ((), ())), preferred_element_type=F32
            )
            return carry

        lax.fori_loop(0, feats // 256, step, 0)
        put_gw.start()

    back = scatter(
        pt,
        lambda y, g: prod2[1 - pt.c, y, g * n : (g + 1) * n, :],
        lambda y, g: prod2[pt.c, y, g * n : (g + 1) * n, :],
        rs2,
        rs2_s,
        sends,
        between=weight_grad,
    )
    part = dh + back
    gx[...] = part
    gx_in[pt.x] = part
    for dev in xpeers:
        remote(gx, gx_in.at[pt.x], tail_s.at[4], tail_s.at[5], dev).start()
    sends.flush()
    put_gw.wait()
    if heads > 1:
        others = gx_in.at[pl.ds(0, heads - 1)]
        arrived(pt, others, tail_s.at[5])
        sends.add(others, tail_s.at[4])
    gh_out[...] = sum(gx_in[k] for k in range(heads))
    sends.flush()


def body(heads, vocab, hidden, res_weight, res_bias, out_weight, targets, loss_mask):
    ny, nz = GRID[vocab]
    rows = hidden.shape[0]
    nvoc, feats = out_weight.shape[1:]
    parts = min(PARTS, nz)
    dma = pltpu.SemaphoreType.DMA
    vm = pltpu.VMEM
    scatter_bufs = [
        vm((ny, nz * FEAT, rows), BF16),
        vm((ny, nz * FEAT, rows), BF16),
        vm((ny - 1, nz * FEAT, rows), BF16),
        vm((ny - 1, nz * FEAT, rows), BF16),
        vm((nz * FEAT, rows), BF16),
        vm((nz, FEAT, rows), BF16),
    ]
    in_vmem = pl.BlockSpec(memory_space=pltpu.VMEM)
    anywhere = pl.BlockSpec(memory_space=pl.ANY)
    gh, gw, gb, loss = pl.pallas_call(
        functools.partial(kernel, heads, vocab),
        out_shape=(
            jax.ShapeDtypeStruct((FEAT, rows), F32),
            jax.ShapeDtypeStruct((FEAT, feats), F32),
            jax.ShapeDtypeStruct((1, FEAT), F32),
            jax.ShapeDtypeStruct((1, 1), F32),
        ),
        in_specs=[anywhere] * 6,
        out_specs=(in_vmem, anywhere, in_vmem, in_vmem),
        scratch_shapes=[
            vm((nvoc, feats), BF16),
            vm((2, ny, nz, FEAT, nvoc), BF16),
            vm((FEAT, feats), BF16),
            vm((2, ny, nz, FEAT, FEAT), BF16),
            vm((2, ny, nz, FEAT, rows), BF16),
            vm((2, ny, nz, FEAT, rows), BF16),
            vm((feats, rows), BF16),
            vm((feats, rows), BF16),
            vm((nvoc, rows), F32),
            vm((nvoc, rows), BF16),
            vm((2, ny, nz * FEAT, rows), F32),
            vm((2, ny, nz * FEAT, rows), F32),
            vm((FEAT, feats), F32),
            vm((8, rows), F32),
            vm((2 * ny, 8, rows), F32),
            vm((8, rows), F32),
            vm((nz, 8, rows), F32),
            vm((FEAT, rows), F32),
            vm((heads, FEAT, rows), F32),
            *scatter_bufs,
            *scatter_bufs,
            vm((ny, nz * FEAT, rows), BF16),
            vm((ny, nz * FEAT, rows), BF16),
            vm((ny, nz * FEAT, rows), BF16),
            vm((ny - 1, nz * FEAT, rows), BF16),
            vm((ny - 1, nz * FEAT, rows), BF16),
            dma((8,)),
            dma((8,)),
            dma((4 + ny + parts,)),
            dma((4 + ny + parts,)),
            dma((4,)),
            dma((6,)),
            dma((7,)),
            vm((1, FEAT), F32),
            vm((1, rows), jnp.int32),
            vm((1, rows), jnp.int32),
        ],
        name="heads_backward",
        compiler_params=pltpu.CompilerParams(
            collective_id=0, has_side_effects=True, vmem_limit_bytes=60 << 20
        ),
    )(hidden.T, res_bias, targets, loss_mask, res_weight[0].T, out_weight[0])
    return gh.T, gw.T[None], gb, loss.reshape(1)


def solution(mesh):
    placed = (
        P(None, "vocab"),
        P("head", None, "vocab"),
        P("head", "vocab"),
        P("head", "vocab", None),
        P("head", None),
        P("head", None),
    )
    return jax.shard_map(
        functools.partial(body, mesh.shape["head"], mesh.shape["vocab"]),
        mesh=mesh,
        in_specs=placed,
        out_specs=(P(None, "vocab"), P("head", None, "vocab"), P("head", "vocab"), P("head")),
        check_vma=False,
    )
```

```python
import functools

import jax
import jax.numpy as jnp
from jax import lax
from jax.experimental import pallas as pl
from jax.experimental.pallas import tpu as pltpu
from jax.sharding import PartitionSpec as P

MESH = pl.DeviceIdType.MESH
F32, BF16 = jnp.float32, jnp.bfloat16
GRID = {128: (4, 16), 16: (2, 4), 8: (2, 2)}
FEAT = 32
PARTS = 4


class Place:
    def __init__(self, heads, vocab):
        self.heads = heads
        self.ny, self.nz = GRID[vocab]
        v = lax.axis_index("vocab")
        self.x = lax.axis_index("head")
        self.v = v
        self.y = lax.div(v, 2 * self.nz)
        self.z = lax.rem(lax.div(v, 2), self.nz)
        self.c = lax.rem(v, 2)
        half = self.nz // 2
        self.dist = sorted(range(self.nz), key=lambda d: (-min(d, self.nz - d), d))
        self.slot_of = {d: j for j, d in enumerate(self.dist)}
        self.half = half
        self.parts = min(PARTS, self.nz)
        self.gs = self.nz // self.parts
        self.reach = self.nz // 4
        self.sib = (self.x, v + 1 - 2 * self.c)
        self.ydist = sorted(range(1, self.ny), key=lambda d: (-min(d, self.ny - d), d))

    def slot(self, z_abs):
        d = lax.rem(z_abs - self.z + self.nz, self.nz)
        return jnp.where(d >= self.half, jnp.where(d == self.half, 0, 2 * (d - self.half)), 2 * (self.half - d) - 1)

    def gather_slot(self, d):
        r = self.reach
        return jnp.where(
            d == 0,
            4 * r - 1,
            jnp.where(
                d <= r,
                3 * r - 2 + d,
                jnp.where(d < 2 * r, d - 1, jnp.where(d < 3 * r, 3 * r - 1 - d, 6 * r - 2 - d)),
            ),
        )

    def yat(self, d):
        return lax.rem(self.y + d + self.ny, self.ny)

    def zat(self, d):
        return lax.rem(self.z + d + self.nz, self.nz)

    def dev(self, y, z, c):
        return (self.x, (y * self.nz + z) * 2 + c)


def remote(src, dst, send, recv, dev):
    return pltpu.make_async_remote_copy(
        src_ref=src, dst_ref=dst, send_sem=send, recv_sem=recv, device_id=dev, device_id_type=MESH
    )


class Sends:
    def __init__(self, pt):
        self.pt = pt
        self.open = []

    def add(self, ref, sem):
        self.open.append((ref, sem))

    def flush(self):
        for ref, sem in self.open:
            remote(ref, ref, sem, sem, self.pt.sib).wait_send()
        self.open = []


def arrived(pt, ref, sem):
    remote(ref, ref, sem, sem, pt.sib).wait_recv()


def gather(pt, buf, sems, sends, between=None):
    zs, ys, cs, cr = (sems.at[k] for k in range(4))
    own = pt.nz - 1
    c = pt.c
    r = pt.reach
    behind, ahead = 2 * r - 1, 3 * r - 1
    groups = ((behind, pt.nz), (0, behind))
    for i in reversed(range(r)):
        for d, there, sem in ((i + 1, behind + i, 4), (-i - 1, ahead + i, 5)):
            remote(buf.at[c, 0, own], buf.at[c, 0, there], zs, sems.at[sem], pt.dev(pt.y, pt.zat(d), c)).start()
    if between is not None:
        between()
    for first, n, there, d, sem in ((behind, r, 0, r, 4), (ahead, r - 1, r, -r, 5)):
        arrived(pt, buf.at[c, 0, pl.ds(first, r)], sems.at[sem])
        if n:
            remote(
                buf.at[c, 0, pl.ds(first, n)],
                buf.at[c, 0, pl.ds(there, n)],
                zs,
                sems.at[6],
                pt.dev(pt.y, pt.zat(d), c),
            ).start()

    def across(rows, lo, hi):
        part = buf.at[c, pl.ds(*rows), pl.ds(lo, hi - lo)]
        remote(part, part, cs, cr, pt.sib).start()

    for g, (lo, hi) in enumerate(groups):
        if g == 1:
            arrived(pt, buf.at[c, 0, pl.ds(lo, hi - lo)], sems.at[6])
        for d in pt.ydist:
            remote(
                buf.at[c, 0, pl.ds(lo, hi - lo)],
                buf.at[c, d, pl.ds(lo, hi - lo)],
                ys,
                sems.at[7 + g],
                pt.dev(pt.yat(d), pt.z, c),
            ).start()
        across((0, 1), lo, hi)
    for g, (lo, hi) in enumerate(groups):
        arrived(pt, buf.at[c, pl.ds(1, pt.ny - 1), pl.ds(lo, hi - lo)], sems.at[7 + g])
        across((1, pt.ny - 1), lo, hi)
    arrived(pt, buf.at[1 - c], cr)
    sends.add(buf.at[c, 0, pl.ds(0, own)], zs)
    sends.add(buf.at[c, pl.ds(1, pt.ny - 1)], ys)
    sends.add(buf.at[c], cs)


def in_order(pt, buf, flat):
    def step(i, carry):
        y, z = lax.div(i, pt.nz), lax.rem(i, pt.nz)
        j = pt.gather_slot(lax.rem(z - pt.z + pt.nz, pt.nz))
        y = lax.rem(pt.y - y + pt.ny, pt.ny)
        for core in range(2):
            flat[pl.ds(pl.multiple_of((i * 2 + core) * FEAT, FEAT), FEAT), :] = buf[core, y, j]
        return carry

    lax.fori_loop(0, pt.ny * pt.nz, step, 0, unroll=4)


def scatter(pt, theirs, mine, bufs, sems, sends, beside=None, between=None, finish=None, late=None):
    to_core, from_core, to_y, from_y, to_z, from_z = bufs
    cs, ys, zs, zr = (sems.at[k] for k in range(4))
    n = pt.gs * FEAT
    last = pt.parts - 1

    def rows(g):
        return pl.ds(g * n, n)

    if beside is not None:
        beside()
    for d in pt.ydist + [0]:
        for g in range(pt.parts):
            to_core[d, rows(g), :] = theirs(pt.yat(d), g).astype(BF16)
        remote(to_core.at[d], from_core.at[d], cs, sems.at[4 + d], pt.sib).start()
    sends.flush()
    sends.add(to_core, cs)
    for g in range(pt.parts):
        for d in pt.ydist:
            if g == 0:
                arrived(pt, from_core.at[d], sems.at[4 + d])
            to_y[d - 1, rows(g), :] = (mine(pt.yat(d), g) + from_core[d, rows(g), :].astype(F32)).astype(BF16)
            remote(
                to_y.at[d - 1, rows(g)],
                from_y.at[d - 1, rows(g)],
                ys,
                sems.at[4 + pt.ny + g],
                pt.dev(pt.yat(d), pt.z, pt.c),
            ).start()
    sends.add(to_y, ys)
    arrived(pt, from_core.at[0], sems.at[4])
    if between is not None:
        between()
    for g in range(pt.parts):
        acc = mine(pt.y, g) + from_core[0, rows(g), :].astype(F32)
        arrived(pt, from_y.at[:, rows(g)], sems.at[4 + pt.ny + g])
        for d in pt.ydist:
            acc = acc + from_y[d - 1, rows(g), :].astype(F32)
        if finish is not None:
            acc = finish(acc, g)
        to_z[rows(g), :] = acc.astype(BF16)
        if g == last:
            total = acc[n - FEAT :, :]
        for j in range(g * pt.gs, (g + 1) * pt.gs):
            if j == pt.nz - 1:
                continue
            d = pt.dist[j]
            there = pt.slot_of[(pt.nz - d) % pt.nz]
            remote(
                to_z.at[pl.ds(j * FEAT, FEAT)], from_z.at[there], zs, zr, pt.dev(pt.y, pt.zat(d), pt.c)
            ).start()
    sends.flush()
    if late is not None:
        late()
    sends.add(to_z.at[pl.ds(0, (pt.nz - 1) * FEAT)], zs)
    arrived(pt, from_z.at[pl.ds(0, pt.nz - 1)], zr)
    for j in range(pt.nz - 1):
        total = total + from_z[j].astype(F32)
    return total


def kernel(heads, vocab, *refs):
    (hid_hbm, bias_hbm, tgt_hbm, msk_hbm, wres_hbm, wout_hbm, gh_out, gw_out, gb_out, loss_out) = refs[:10]
    (wo, wot, wr, wrt, buf1, buf2, flat1, flat2, logits, eo, prod, prod2, gw, st, st_y, sz, st_z, gx, gx_in) = refs[10:29]
    rs1, rs2 = refs[29:35], refs[35:41]
    t_to_core, t_from_core, t_mine, t_to_y, t_from_y = refs[41:46]
    ag1_s, ag2_s, rs1_s, rs2_s, t_s, tail_s, local = refs[46:53]
    bias, tgt, msk = refs[53:56]
    pt = Place(heads, vocab)
    ny, nz = pt.ny, pt.nz
    nrow = buf1.shape[-1]
    nvoc = wo.shape[0]
    feats = wo.shape[1]
    ychunk = feats // ny
    sends = Sends(pt)

    hid = buf1.at[pt.c, 0, nz - 1]
    get_wr = pltpu.make_async_copy(wres_hbm, wr, local.at[0])
    get_wo = pltpu.make_async_copy(wout_hbm, wo, local.at[1])
    get_hid = pltpu.make_async_copy(hid_hbm, hid, local.at[3])
    get_small = [
        pltpu.make_async_copy(src, dst, local.at[4 + k])
        for k, (src, dst) in enumerate(((bias_hbm, bias), (tgt_hbm, tgt), (msk_hbm, msk)))
    ]
    for cp in [get_hid, get_wr, *get_small, get_wo]:
        cp.start()

    peers = [pt.dev(pt.y, pt.zat(d), pt.c) for k in range(pt.reach, 0, -1) for d in (k, -k)]
    plane = [(dy, dc) for dy in range(ny) for dc in range(2) if dy or dc]
    near = [pt.dev(pt.yat(dy), pt.z, lax.rem(pt.c + dc, 2)) for dy, dc in plane]
    xpeers = [(lax.rem(pt.x + d, heads), pt.v) for d in range(1, heads)]
    barrier = pltpu.get_barrier_semaphore()
    for dev in peers + near + xpeers:
        pl.semaphore_signal(barrier, inc=1, device_id=dev, device_id_type=MESH)

    per = 256 // (2 * FEAT)

    def place_rows(dst, chunk, i):
        y = lax.div(i * per, nz)
        z0 = lax.rem(i * per, nz)
        for k in range(per):
            j = pt.slot(z0 + k)
            for core in range(2):
                r = (k * 2 + core) * FEAT
                dst[core, y, j] = chunk[r : r + FEAT, :]

    def turn_wr(i, carry):
        place_rows(wrt, wr[:, pl.ds(pl.multiple_of(i * 256, 256), 256)].T, i)
        return carry

    for cp in get_small:
        cp.wait()
    get_hid.wait()
    pl.semaphore_wait(barrier, len(peers) + len(near) + len(xpeers))

    def turn_wo(i, carry):
        place_rows(wot, wo[:, pl.ds(pl.multiple_of(i * 256, 256), 256)].T, i)
        return carry

    def turn():
        get_wr.wait()
        lax.fori_loop(0, feats // 256, turn_wr, 0)
        get_wo.wait()
        lax.fori_loop(0, feats // 256, turn_wo, 0)

    ids = pt.v * nvoc + lax.broadcasted_iota(jnp.int32, (nvoc, nrow), 0)

    def rows_of(core, y):
        w = wot[core, y].reshape(nz * FEAT, nvoc)
        return jnp.dot(w, eo[...], preferred_element_type=F32).astype(BF16)

    def prepare():
        turn()
        eo[...] = (ids == tgt[...]).astype(BF16)
        for d in range(ny):
            t_to_core[d] = rows_of(1 - pt.c, pt.yat(d))
        remote(t_to_core, t_from_core, t_s.at[0], t_s.at[1], pt.sib).start()
        sends.add(t_to_core, t_s.at[0])
        for d in range(ny):
            t_mine[d] = rows_of(pt.c, pt.yat(d))

    gather(pt, buf1, ag1_s, sends, prepare)
    in_order(pt, buf1, flat1)

    eye = lax.broadcasted_iota(jnp.int32, (FEAT, FEAT), 0) == lax.broadcasted_iota(jnp.int32, (FEAT, FEAT), 1)
    bias_col = jnp.sum(jnp.where(eye, bias[...], 0.0), axis=1, keepdims=True)
    pre = jnp.zeros((FEAT, nrow), F32)
    for y in range(ny):
        pre = pre + jnp.dot(
            wr[:, y * ychunk : (y + 1) * ychunk], flat1[y * ychunk : (y + 1) * ychunk, :], preferred_element_type=F32
        )
    pre = pre + bias_col
    sig = jax.nn.sigmoid(pre)
    buf2[pt.c, 0, nz - 1] = (hid[...].astype(F32) + pre * sig).astype(BF16)
    gate = sig * (1.0 + pre * (1.0 - sig))


    def target_rows():
        arrived(pt, t_from_core, t_s.at[1])
        for d in pt.ydist:
            t_to_y[d - 1] = t_mine[d] + t_from_core[d]
            remote(t_to_y.at[d - 1], t_from_y.at[d - 1], t_s.at[2], t_s.at[3], pt.dev(pt.yat(d), pt.z, pt.c)).start()
        sends.flush()
        sends.add(t_to_y, t_s.at[2])

    gather(pt, buf2, ag2_s, sends, target_rows)
    in_order(pt, buf2, flat2)

    logits[...] = jnp.zeros_like(logits)

    def logit_step(i, carry):
        at = pl.ds(pl.multiple_of(i * ychunk, ychunk), ychunk)
        logits[...] += jnp.dot(wo[:, at], flat2[at, :], preferred_element_type=F32)
        return carry

    lax.fori_loop(0, ny, logit_step, 0)
    hit = ids == tgt[...]
    lg = logits[...]
    top = jnp.max(lg, axis=0, keepdims=True)
    picked = jnp.sum(jnp.where(hit, lg, 0.0), axis=0, keepdims=True)
    e = jnp.exp(lg - top)
    e_hit = jnp.sum(jnp.where(hit, e, 0.0), axis=0, keepdims=True)
    e = jnp.where(hit, 0.0, e)
    rest = jnp.sum(e, axis=0, keepdims=True)
    eo[...] = e.astype(BF16)

    def pack(*values):
        r = lax.broadcasted_iota(jnp.int32, (8, nrow), 0)
        out = jnp.zeros((8, nrow), F32)
        for k, value in enumerate(values):
            out = jnp.where(r == k, value, out)
        return out

    def merge(ref, count):
        tops = [ref[i, 0:1, :] for i in range(count)]
        best = functools.reduce(jnp.maximum, tops)
        scale = [jnp.exp(t - best) for t in tops]
        others = sum(ref[i, 1:2, :] * scale[i] for i in range(count))
        target = sum(ref[i, 2:3, :] * scale[i] for i in range(count))
        pick = sum(ref[i, 3:4, :] for i in range(count))
        return best, others, target, pick

    packed = pack(top, rest, e_hit, picked)
    st[...] = packed
    me = pt.y * 2 + pt.c
    st_y[me] = packed
    for dev in near:
        remote(st, st_y.at[me], tail_s.at[0], tail_s.at[1], dev).start()

    def product(i, carry):
        core, y = lax.div(i, ny), lax.rem(i, ny)
        prod[core, y] = jnp.dot(wot[core, y].reshape(nz * FEAT, nvoc), eo[...], preferred_element_type=F32)
        return carry

    lax.fori_loop(0, 2 * ny, product, 0)
    arrived(pt, st_y.at[pl.ds(0, 2 * ny - 1)], tail_s.at[1])
    sends.add(st_y.at[pl.ds(0, 2 * ny - 1)], tail_s.at[0])
    plane_stats = merge(st_y, 2 * ny)
    plane_top = plane_stats[0]
    scale = jnp.exp(top - plane_top)
    n = pt.gs * FEAT

    def stats_out():
        packed = pack(*plane_stats)
        sz[...] = packed
        st_z[pt.z] = packed
        for d in pt.dist[:-1]:
            remote(sz, st_z.at[pt.z], tail_s.at[2], tail_s.at[3], pt.dev(pt.y, pt.zat(d), pt.c)).start()

    factors = []

    def stats_in():
        arrived(pt, st_z.at[pl.ds(0, nz - 1)], tail_s.at[3])
        sends.add(st_z.at[pl.ds(0, nz - 1)], tail_s.at[2])
        best, others, target, pick = merge(st_z, nz)
        total = others + target
        lse = best + jnp.log(total)
        factor = jnp.float32(0.8**heads)
        for k in range(heads - 1):
            factor = jnp.where(pt.x == k, jnp.float32(0.8 ** (k + 1)), factor)
        weight = factor * msk[...].astype(F32) / nrow
        loss_out[...] = jnp.sum(weight * (lse - pick), axis=1, keepdims=True)
        alpha = weight * jnp.exp(plane_top - lse)
        beta = (-weight * (others / total)).astype(BF16).astype(F32)
        factors.extend((alpha, beta))
        arrived(pt, t_from_y, t_s.at[3])

    def finish(acc, g):
        alpha, beta = factors
        at = pl.ds(g * n, n)
        rows = t_mine[0, at, :].astype(F32) + t_from_core[0, at, :].astype(F32)
        for d in pt.ydist:
            rows = rows + t_from_y[d - 1, at, :].astype(F32)
        return alpha * acc + beta * rows

    dh = scatter(
        pt,
        lambda y, g: scale * prod[1 - pt.c, y, g * n : (g + 1) * n, :],
        lambda y, g: scale * prod[pt.c, y, g * n : (g + 1) * n, :],
        rs1,
        rs1_s,
        sends,
        stats_out,
        stats_in,
        finish,
    )
    dpre = (dh * gate).astype(BF16)
    gb = jnp.sum(dpre.astype(F32), axis=1, keepdims=True)
    gb_out[...] = jnp.sum(jnp.where(eye, gb, 0.0), axis=0, keepdims=True)

    for core in range(2):
        for y in range(ny):
            prod2[core, y] = jnp.dot(
                wrt[core, y].reshape(nz * FEAT, FEAT), dpre, preferred_element_type=F32
            )
    put_gw = pltpu.make_async_copy(gw, gw_out, local.at[2])

    def weight_grad():
        def step(i, carry):
            at = pl.ds(pl.multiple_of(i * 256, 256), 256)
            gw[:, at] = lax.dot_general(
                dpre, flat1[at, :], (((1,), (1,)), ((), ())), preferred_element_type=F32
            )
            return carry

        lax.fori_loop(0, feats // 256, step, 0)
        put_gw.start()

    back = scatter(
        pt,
        lambda y, g: prod2[1 - pt.c, y, g * n : (g + 1) * n, :],
        lambda y, g: prod2[pt.c, y, g * n : (g + 1) * n, :],
        rs2,
        rs2_s,
        sends,
        late=weight_grad,
    )
    part = dh + back
    gx[...] = part
    gx_in[pt.x] = part
    for dev in xpeers:
        remote(gx, gx_in.at[pt.x], tail_s.at[4], tail_s.at[5], dev).start()
    sends.flush()
    put_gw.wait()
    if heads > 1:
        others = gx_in.at[pl.ds(0, heads - 1)]
        arrived(pt, others, tail_s.at[5])
        sends.add(others, tail_s.at[4])
    gh_out[...] = sum(gx_in[k] for k in range(heads))
    sends.flush()


def body(heads, vocab, hidden, res_weight, res_bias, out_weight, targets, loss_mask):
    ny, nz = GRID[vocab]
    rows = hidden.shape[0]
    nvoc, feats = out_weight.shape[1:]
    parts = min(PARTS, nz)
    dma = pltpu.SemaphoreType.DMA
    vm = pltpu.VMEM
    scatter_bufs = [
        vm((ny, nz * FEAT, rows), BF16),
        vm((ny, nz * FEAT, rows), BF16),
        vm((ny - 1, nz * FEAT, rows), BF16),
        vm((ny - 1, nz * FEAT, rows), BF16),
        vm((nz * FEAT, rows), BF16),
        vm((nz, FEAT, rows), BF16),
    ]
    in_vmem = pl.BlockSpec(memory_space=pltpu.VMEM)
    anywhere = pl.BlockSpec(memory_space=pl.ANY)
    gh, gw, gb, loss = pl.pallas_call(
        functools.partial(kernel, heads, vocab),
        out_shape=(
            jax.ShapeDtypeStruct((FEAT, rows), F32),
            jax.ShapeDtypeStruct((FEAT, feats), F32),
            jax.ShapeDtypeStruct((1, FEAT), F32),
            jax.ShapeDtypeStruct((1, 1), F32),
        ),
        in_specs=[anywhere] * 6,
        out_specs=(in_vmem, anywhere, in_vmem, in_vmem),
        scratch_shapes=[
            vm((nvoc, feats), BF16),
            vm((2, ny, nz, FEAT, nvoc), BF16),
            vm((FEAT, feats), BF16),
            vm((2, ny, nz, FEAT, FEAT), BF16),
            vm((2, ny, nz, FEAT, rows), BF16),
            vm((2, ny, nz, FEAT, rows), BF16),
            vm((feats, rows), BF16),
            vm((feats, rows), BF16),
            vm((nvoc, rows), F32),
            vm((nvoc, rows), BF16),
            vm((2, ny, nz * FEAT, rows), F32),
            vm((2, ny, nz * FEAT, rows), F32),
            vm((FEAT, feats), F32),
            vm((8, rows), F32),
            vm((2 * ny, 8, rows), F32),
            vm((8, rows), F32),
            vm((nz, 8, rows), F32),
            vm((FEAT, rows), F32),
            vm((heads, FEAT, rows), F32),
            *scatter_bufs,
            *scatter_bufs,
            vm((ny, nz * FEAT, rows), BF16),
            vm((ny, nz * FEAT, rows), BF16),
            vm((ny, nz * FEAT, rows), BF16),
            vm((ny - 1, nz * FEAT, rows), BF16),
            vm((ny - 1, nz * FEAT, rows), BF16),
            dma((9,)),
            dma((9,)),
            dma((4 + ny + parts,)),
            dma((4 + ny + parts,)),
            dma((4,)),
            dma((6,)),
            dma((7,)),
            vm((1, FEAT), F32),
            vm((1, rows), jnp.int32),
            vm((1, rows), jnp.int32),
        ],
        name="heads_backward",
        compiler_params=pltpu.CompilerParams(
            collective_id=0, has_side_effects=True, vmem_limit_bytes=60 << 20
        ),
    )(hidden.T, res_bias, targets, loss_mask, res_weight[0].T, out_weight[0])
    return gh.T, gw.T[None], gb, loss.reshape(1)


def solution(mesh):
    placed = (
        P(None, "vocab"),
        P("head", None, "vocab"),
        P("head", "vocab"),
        P("head", "vocab", None),
        P("head", None),
        P("head", None),
    )
    return jax.shard_map(
        functools.partial(body, mesh.shape["head"], mesh.shape["vocab"]),
        mesh=mesh,
        in_specs=placed,
        out_specs=(P(None, "vocab"), P("head", None, "vocab"), P("head", "vocab"), P("head")),
        check_vma=False,
    )
```

```python
import functools

import jax
import jax.numpy as jnp
from jax import lax
from jax.experimental import pallas as pl
from jax.experimental.pallas import tpu as pltpu
from jax.sharding import PartitionSpec as P

MESH = pl.DeviceIdType.MESH
F32, BF16 = jnp.float32, jnp.bfloat16
GRID = {128: (4, 16), 16: (2, 4), 8: (2, 2)}
FEAT = 32
PARTS = 8


class Place:
    def __init__(self, heads, vocab):
        self.heads = heads
        self.ny, self.nz = GRID[vocab]
        v = lax.axis_index("vocab")
        self.x = lax.axis_index("head")
        self.v = v
        self.y = lax.div(v, 2 * self.nz)
        self.z = lax.rem(lax.div(v, 2), self.nz)
        self.c = lax.rem(v, 2)
        half = self.nz // 2
        self.dist = sorted(range(self.nz), key=lambda d: (-min(d, self.nz - d), d))
        self.slot_of = {d: j for j, d in enumerate(self.dist)}
        self.half = half
        self.parts = min(PARTS, self.nz)
        self.gs = self.nz // self.parts
        self.reach = self.nz // 4
        self.sib = (self.x, v + 1 - 2 * self.c)
        self.ydist = sorted(range(1, self.ny), key=lambda d: (-min(d, self.ny - d), d))

    def slot(self, z_abs):
        d = lax.rem(z_abs - self.z + self.nz, self.nz)
        return jnp.where(d >= self.half, jnp.where(d == self.half, 0, 2 * (d - self.half)), 2 * (self.half - d) - 1)

    def gather_slot(self, d):
        r = self.reach
        return jnp.where(
            d == 0,
            4 * r - 1,
            jnp.where(
                d <= r,
                3 * r - 2 + d,
                jnp.where(d < 2 * r, d - 1, jnp.where(d < 3 * r, 3 * r - 1 - d, 6 * r - 2 - d)),
            ),
        )

    def yat(self, d):
        return lax.rem(self.y + d + self.ny, self.ny)

    def zat(self, d):
        return lax.rem(self.z + d + self.nz, self.nz)

    def dev(self, y, z, c):
        return (self.x, (y * self.nz + z) * 2 + c)


def remote(src, dst, send, recv, dev):
    return pltpu.make_async_remote_copy(
        src_ref=src, dst_ref=dst, send_sem=send, recv_sem=recv, device_id=dev, device_id_type=MESH
    )


class Sends:
    def __init__(self, pt):
        self.pt = pt
        self.open = []

    def add(self, ref, sem):
        self.open.append((ref, sem))

    def flush(self):
        for ref, sem in self.open:
            remote(ref, ref, sem, sem, self.pt.sib).wait_send()
        self.open = []


def arrived(pt, ref, sem):
    remote(ref, ref, sem, sem, pt.sib).wait_recv()


def gather(pt, buf, sems, sends, between=None, late=None):
    zs, ys, cs, cr = (sems.at[k] for k in range(4))
    own = pt.nz - 1
    c = pt.c
    r = pt.reach
    behind, ahead = 2 * r - 1, 3 * r - 1
    groups = ((behind, pt.nz), (0, behind))
    for i in reversed(range(r)):
        for d, there, sem in ((i + 1, behind + i, 4), (-i - 1, ahead + i, 5)):
            remote(buf.at[c, 0, own], buf.at[c, 0, there], zs, sems.at[sem], pt.dev(pt.y, pt.zat(d), c)).start()
    if between is not None:
        between()
    for first, n, there, d, sem in ((behind, r, 0, r, 4), (ahead, r - 1, r, -r, 5)):
        arrived(pt, buf.at[c, 0, pl.ds(first, r)], sems.at[sem])
        if n:
            remote(
                buf.at[c, 0, pl.ds(first, n)],
                buf.at[c, 0, pl.ds(there, n)],
                zs,
                sems.at[6],
                pt.dev(pt.y, pt.zat(d), c),
            ).start()

    def across(rows, lo, hi):
        part = buf.at[c, pl.ds(*rows), pl.ds(lo, hi - lo)]
        remote(part, part, cs, cr, pt.sib).start()

    for g, (lo, hi) in enumerate(groups):
        if g == 1:
            arrived(pt, buf.at[c, 0, pl.ds(lo, hi - lo)], sems.at[6])
        for d in pt.ydist:
            remote(
                buf.at[c, 0, pl.ds(lo, hi - lo)],
                buf.at[c, d, pl.ds(lo, hi - lo)],
                ys,
                sems.at[7 + g],
                pt.dev(pt.yat(d), pt.z, c),
            ).start()
        across((0, 1), lo, hi)
    for g, (lo, hi) in enumerate(groups):
        arrived(pt, buf.at[c, pl.ds(1, pt.ny - 1), pl.ds(lo, hi - lo)], sems.at[7 + g])
        across((1, pt.ny - 1), lo, hi)
        if g == 0 and late is not None:
            late()
    arrived(pt, buf.at[1 - c], cr)
    sends.add(buf.at[c, 0, pl.ds(0, own)], zs)
    sends.add(buf.at[c, pl.ds(1, pt.ny - 1)], ys)
    sends.add(buf.at[c], cs)


def in_order(pt, buf, flat):
    def step(i, carry):
        y, z = lax.div(i, pt.nz), lax.rem(i, pt.nz)
        j = pt.gather_slot(lax.rem(z - pt.z + pt.nz, pt.nz))
        y = lax.rem(pt.y - y + pt.ny, pt.ny)
        for core in range(2):
            flat[pl.ds(pl.multiple_of((i * 2 + core) * FEAT, FEAT), FEAT), :] = buf[core, y, j]
        return carry

    lax.fori_loop(0, pt.ny * pt.nz, step, 0, unroll=4)


def send_along_z(pt, src, dst, j, send, recv):
    d = pt.dist[j]
    there = pt.slot_of[(pt.nz - d) % pt.nz]
    remote(
        src.at[pl.ds(j * FEAT, FEAT)], dst.at[there], send, recv, pt.dev(pt.y, pt.zat(d), pt.c)
    ).start()


def scatter(pt, term, own, bufs, sems, sends, ready=None, beside=None, late=None, combine=None):
    to_core, from_core, to_y, from_y, to_z, from_z = bufs
    cs, ys, zs, zr = (sems.at[k] for k in range(4))
    n = pt.gs * FEAT
    last = pt.parts - 1

    def rows(g):
        return pl.ds(g * n, n)

    for d in pt.ydist + [0]:
        to_core[d] = term(1 - pt.c, pt.yat(d)).astype(BF16)
        remote(to_core.at[d], from_core.at[d], cs, sems.at[4 + d], pt.sib).start()
    for d in pt.ydist + [0]:
        own[d] = term(pt.c, pt.yat(d))
    sends.flush()
    sends.add(to_core, cs)
    factors = ready() if ready is not None else None

    def both(d, g):
        mine, other = own[d, rows(g), :], from_core[d, rows(g), :].astype(F32)
        return mine + other if factors is None else factors[0] * mine + factors[1] * other

    for g in range(pt.parts):
        for d in pt.ydist:
            if g == 0:
                arrived(pt, from_core.at[d], sems.at[4 + d])
            to_y[d - 1, rows(g), :] = both(d, g).astype(BF16)
            remote(
                to_y.at[d - 1, rows(g)],
                from_y.at[d - 1, rows(g)],
                ys,
                sems.at[4 + pt.ny + g],
                pt.dev(pt.yat(d), pt.z, pt.c),
            ).start()
    sends.add(to_y, ys)
    arrived(pt, from_core.at[0], sems.at[4])
    if beside is not None:
        beside()
    for g in range(pt.parts):
        acc = both(0, g)
        arrived(pt, from_y.at[:, rows(g)], sems.at[4 + pt.ny + g])
        for d in pt.ydist:
            acc = acc + from_y[d - 1, rows(g), :].astype(F32)
        to_z[rows(g), :] = acc.astype(BF16)
        if g == last:
            total = acc[n - FEAT :, :]
        for j in range(g * pt.gs, min((g + 1) * pt.gs, pt.nz - 1)):
            send_along_z(pt, to_z, from_z, j, zs, zr)
    sends.flush()
    if late is not None:
        late()
    sends.add(to_z.at[pl.ds(0, (pt.nz - 1) * FEAT)], zs)
    arrived(pt, from_z.at[pl.ds(0, pt.nz - 1)], zr)
    others = [from_z[j].astype(F32) for j in range(pt.nz - 1)]
    return sum(others, total) if combine is None else combine(total, others)


def kernel(heads, vocab, *refs):
    (hid_hbm, bias_hbm, tgt_hbm, msk_hbm, wres_hbm, wout_hbm, gh_out, gw_out, gb_out, loss_out) = refs[:10]
    (wo, wot, wr, wrt, buf1, buf2, flat1, flat2, logits, eo, hits, own, gw, st, st_y, sz, st_z, gx, gx_in) = refs[10:29]
    rs1, rs2 = refs[29:35], refs[35:41]
    t_to_core, t_from_core, t_mine, t_to_y, t_from_y, t_to_z, t_from_z = refs[41:48]
    ag1_s, ag2_s, rs1_s, rs2_s, t_s, tail_s, local = refs[48:55]
    bias, tgt, msk = refs[55:58]
    pt = Place(heads, vocab)
    ny, nz = pt.ny, pt.nz
    nrow = buf1.shape[-1]
    nvoc = wo.shape[0]
    feats = wo.shape[1]
    ychunk = feats // ny
    sends = Sends(pt)

    hid = buf1.at[pt.c, 0, nz - 1]
    get_wr = pltpu.make_async_copy(wres_hbm, wr, local.at[0])
    get_wo = pltpu.make_async_copy(wout_hbm, wo, local.at[1])
    get_hid = pltpu.make_async_copy(hid_hbm, hid, local.at[3])
    get_small = [
        pltpu.make_async_copy(src, dst, local.at[4 + k])
        for k, (src, dst) in enumerate(((bias_hbm, bias), (tgt_hbm, tgt), (msk_hbm, msk)))
    ]
    for cp in [get_hid, get_wr, *get_small, get_wo]:
        cp.start()

    peers = [pt.dev(pt.y, pt.zat(d), pt.c) for k in range(pt.reach, 0, -1) for d in (k, -k)]
    plane = [(dy, dc) for dy in range(ny) for dc in range(2) if dy or dc]
    near = [pt.dev(pt.yat(dy), pt.z, lax.rem(pt.c + dc, 2)) for dy, dc in plane]
    xpeers = [(lax.rem(pt.x + d, heads), pt.v) for d in range(1, heads)]
    barrier = pltpu.get_barrier_semaphore()
    for dev in peers + near + xpeers:
        pl.semaphore_signal(barrier, inc=1, device_id=dev, device_id_type=MESH)

    per = 256 // (2 * FEAT)

    def place_rows(dst, chunk, i):
        y = lax.div(i * per, nz)
        z0 = lax.rem(i * per, nz)
        for k in range(per):
            j = pt.slot(z0 + k)
            for core in range(2):
                r = (k * 2 + core) * FEAT
                dst[core, y, j] = chunk[r : r + FEAT, :]

    def turn_wr(i, carry):
        place_rows(wrt, wr[:, pl.ds(pl.multiple_of(i * 256, 256), 256)].T, i)
        return carry

    for cp in get_small:
        cp.wait()
    get_hid.wait()
    pl.semaphore_wait(barrier, len(peers) + len(near) + len(xpeers))

    def turn_wo(i, carry):
        place_rows(wot, wo[:, pl.ds(pl.multiple_of(i * 256, 256), 256)].T, i)
        return carry

    def turn():
        get_wr.wait()
        lax.fori_loop(0, feats // 256, turn_wr, 0)
        get_wo.wait()
        lax.fori_loop(0, feats // 256, turn_wo, 0)

    ids = pt.v * nvoc + lax.broadcasted_iota(jnp.int32, (nvoc, nrow), 0)

    def rows_of(core, y):
        w = wot[core, y].reshape(nz * FEAT, nvoc)
        return jnp.dot(w, hits[...], preferred_element_type=F32).astype(BF16)

    def prepare():
        hits[...] = (ids == tgt[...]).astype(BF16)
        for d in range(ny):
            t_to_core[d] = rows_of(1 - pt.c, pt.yat(d))
        remote(t_to_core, t_from_core, t_s.at[0], t_s.at[1], pt.sib).start()
        sends.add(t_to_core, t_s.at[0])
        for d in range(ny):
            t_mine[d] = rows_of(pt.c, pt.yat(d))

    gather(pt, buf1, ag1_s, sends, turn, prepare)
    in_order(pt, buf1, flat1)

    eye = lax.broadcasted_iota(jnp.int32, (FEAT, FEAT), 0) == lax.broadcasted_iota(jnp.int32, (FEAT, FEAT), 1)
    bias_col = jnp.sum(jnp.where(eye, bias[...], 0.0), axis=1, keepdims=True)
    pre = jnp.zeros((FEAT, nrow), F32)
    for y in range(ny):
        pre = pre + jnp.dot(
            wr[:, y * ychunk : (y + 1) * ychunk], flat1[y * ychunk : (y + 1) * ychunk, :], preferred_element_type=F32
        )
    pre = pre + bias_col
    sig = jax.nn.sigmoid(pre)
    buf2[pt.c, 0, nz - 1] = (hid[...].astype(F32) + pre * sig).astype(BF16)
    gate = sig * (1.0 + pre * (1.0 - sig))


    def target_rows():
        arrived(pt, t_from_core, t_s.at[1])
        for d in pt.ydist:
            t_to_y[d - 1] = t_mine[d] + t_from_core[d]
            remote(t_to_y.at[d - 1], t_from_y.at[d - 1], t_s.at[2], t_s.at[3], pt.dev(pt.yat(d), pt.z, pt.c)).start()
        sends.flush()
        sends.add(t_to_y, t_s.at[2])

    def target_rows_z():
        arrived(pt, t_from_y, t_s.at[3])
        rows = t_mine[0] + t_from_core[0]
        for d in pt.ydist:
            rows = rows + t_from_y[d - 1]
        t_to_z[...] = rows
        for j in range(nz - 1):
            send_along_z(pt, t_to_z, t_from_z, j, t_s.at[4], t_s.at[5])
        sends.add(t_to_z.at[pl.ds(0, (nz - 1) * FEAT)], t_s.at[4])

    gather(pt, buf2, ag2_s, sends, target_rows, target_rows_z)
    in_order(pt, buf2, flat2)

    logits[...] = jnp.zeros_like(logits)

    def logit_step(i, carry):
        at = pl.ds(pl.multiple_of(i * ychunk, ychunk), ychunk)
        logits[...] += jnp.dot(wo[:, at], flat2[at, :], preferred_element_type=F32)
        return carry

    lax.fori_loop(0, ny, logit_step, 0)
    hit = ids == tgt[...]
    lg = logits[...]
    top = jnp.max(lg, axis=0, keepdims=True)
    picked = jnp.sum(jnp.where(hit, lg, 0.0), axis=0, keepdims=True)
    e = jnp.exp(lg - top)
    e_hit = jnp.sum(jnp.where(hit, e, 0.0), axis=0, keepdims=True)
    e = jnp.where(hit, 0.0, e)
    rest = jnp.sum(e, axis=0, keepdims=True)
    eo[...] = e.astype(BF16)

    def pack(*values):
        r = lax.broadcasted_iota(jnp.int32, (8, nrow), 0)
        out = jnp.zeros((8, nrow), F32)
        for k, value in enumerate(values):
            out = jnp.where(r == k, value, out)
        return out

    def merge(ref, count):
        tops = [ref[i, 0:1, :] for i in range(count)]
        best = functools.reduce(jnp.maximum, tops)
        scale = [jnp.exp(t - best) for t in tops]
        others = sum(ref[i, 1:2, :] * scale[i] for i in range(count))
        target = sum(ref[i, 2:3, :] * scale[i] for i in range(count))
        pick = sum(ref[i, 3:4, :] for i in range(count))
        return best, others, target, pick

    packed = pack(top, rest, e_hit, picked)
    st[...] = packed
    me = pt.y * 2 + pt.c
    st_y[me] = packed
    for dev in near:
        remote(st, st_y.at[me], tail_s.at[0], tail_s.at[1], dev).start()

    plane_stats = []

    def stats_near():
        arrived(pt, st_y.at[pl.ds(0, 2 * ny - 1)], tail_s.at[1])
        sends.add(st_y.at[pl.ds(0, 2 * ny - 1)], tail_s.at[0])
        plane_stats.extend(merge(st_y, 2 * ny))
        return jnp.exp(top - plane_stats[0]), jnp.exp(st_y[me + 1 - 2 * pt.c, 0:1, :] - plane_stats[0])

    def stats_out():
        packed = pack(*plane_stats)
        sz[...] = packed
        st_z[pt.z] = packed
        for d in pt.dist[:-1]:
            remote(sz, st_z.at[pt.z], tail_s.at[2], tail_s.at[3], pt.dev(pt.y, pt.zat(d), pt.c)).start()

    def weigh(mine, others):
        arrived(pt, st_z.at[pl.ds(0, nz - 1)], tail_s.at[3])
        sends.add(st_z.at[pl.ds(0, nz - 1)], tail_s.at[2])
        best, rest, target, pick = merge(st_z, nz)
        total = rest + target
        lse = best + jnp.log(total)
        factor = jnp.float32(0.8**heads)
        for k in range(heads - 1):
            factor = jnp.where(pt.x == k, jnp.float32(0.8 ** (k + 1)), factor)
        weight = factor * msk[...].astype(F32) / nrow
        loss_out[...] = jnp.sum(weight * (lse - pick), axis=1, keepdims=True)
        beta = (-weight * (rest / total)).astype(BF16).astype(F32)
        arrived(pt, t_from_z.at[pl.ds(0, nz - 1)], t_s.at[5])
        rows = t_to_z[(nz - 1) * FEAT :, :].astype(F32)
        out = jnp.exp(plane_stats[0] - lse) * mine
        for j in range(nz - 1):
            rows = rows + t_from_z[j].astype(F32)
            out = out + jnp.exp(st_z[pt.zat(pt.dist[j]), 0:1, :] - lse) * others[j]
        return weight * out + beta * rows

    def vocab_term(core, y):
        return jnp.dot(wot[core, y].reshape(nz * FEAT, nvoc), eo[...], preferred_element_type=F32)

    dh = scatter(pt, vocab_term, own, rs1, rs1_s, sends, stats_near, stats_out, None, weigh)
    dpre = (dh * gate).astype(BF16)
    gb = jnp.sum(dpre.astype(F32), axis=1, keepdims=True)
    gb_out[...] = jnp.sum(jnp.where(eye, gb, 0.0), axis=0, keepdims=True)

    put_gw = pltpu.make_async_copy(gw, gw_out, local.at[2])

    def weight_grad():
        def step(i, carry):
            at = pl.ds(pl.multiple_of(i * 256, 256), 256)
            gw[:, at] = lax.dot_general(
                dpre, flat1[at, :], (((1,), (1,)), ((), ())), preferred_element_type=F32
            )
            return carry

        lax.fori_loop(0, feats // 256, step, 0)
        put_gw.start()

    def residual_term(core, y):
        return jnp.dot(wrt[core, y].reshape(nz * FEAT, FEAT), dpre, preferred_element_type=F32)

    back = scatter(pt, residual_term, own, rs2, rs2_s, sends, late=weight_grad)
    part = dh + back
    gx[...] = part
    gx_in[pt.x] = part
    for dev in xpeers:
        remote(gx, gx_in.at[pt.x], tail_s.at[4], tail_s.at[5], dev).start()
    sends.flush()
    put_gw.wait()
    if heads > 1:
        others = gx_in.at[pl.ds(0, heads - 1)]
        arrived(pt, others, tail_s.at[5])
        sends.add(others, tail_s.at[4])
    gh_out[...] = sum(gx_in[k] for k in range(heads))
    sends.flush()


def body(heads, vocab, hidden, res_weight, res_bias, out_weight, targets, loss_mask):
    ny, nz = GRID[vocab]
    rows = hidden.shape[0]
    nvoc, feats = out_weight.shape[1:]
    parts = min(PARTS, nz)
    dma = pltpu.SemaphoreType.DMA
    vm = pltpu.VMEM
    scatter_bufs = [
        vm((ny, nz * FEAT, rows), BF16),
        vm((ny, nz * FEAT, rows), BF16),
        vm((ny - 1, nz * FEAT, rows), BF16),
        vm((ny - 1, nz * FEAT, rows), BF16),
        vm((nz * FEAT, rows), BF16),
        vm((nz, FEAT, rows), BF16),
    ]
    in_vmem = pl.BlockSpec(memory_space=pltpu.VMEM)
    anywhere = pl.BlockSpec(memory_space=pl.ANY)
    gh, gw, gb, loss = pl.pallas_call(
        functools.partial(kernel, heads, vocab),
        out_shape=(
            jax.ShapeDtypeStruct((FEAT, rows), F32),
            jax.ShapeDtypeStruct((FEAT, feats), F32),
            jax.ShapeDtypeStruct((1, FEAT), F32),
            jax.ShapeDtypeStruct((1, 1), F32),
        ),
        in_specs=[anywhere] * 6,
        out_specs=(in_vmem, anywhere, in_vmem, in_vmem),
        scratch_shapes=[
            vm((nvoc, feats), BF16),
            vm((2, ny, nz, FEAT, nvoc), BF16),
            vm((FEAT, feats), BF16),
            vm((2, ny, nz, FEAT, FEAT), BF16),
            vm((2, ny, nz, FEAT, rows), BF16),
            vm((2, ny, nz, FEAT, rows), BF16),
            vm((feats, rows), BF16),
            vm((feats, rows), BF16),
            vm((nvoc, rows), F32),
            vm((nvoc, rows), BF16),
            vm((nvoc, rows), BF16),
            vm((ny, nz * FEAT, rows), F32),
            vm((FEAT, feats), F32),
            vm((8, rows), F32),
            vm((2 * ny, 8, rows), F32),
            vm((8, rows), F32),
            vm((nz, 8, rows), F32),
            vm((FEAT, rows), F32),
            vm((heads, FEAT, rows), F32),
            *scatter_bufs,
            *scatter_bufs,
            vm((ny, nz * FEAT, rows), BF16),
            vm((ny, nz * FEAT, rows), BF16),
            vm((ny, nz * FEAT, rows), BF16),
            vm((ny - 1, nz * FEAT, rows), BF16),
            vm((ny - 1, nz * FEAT, rows), BF16),
            vm((nz * FEAT, rows), BF16),
            vm((nz, FEAT, rows), BF16),
            dma((9,)),
            dma((9,)),
            dma((4 + ny + parts,)),
            dma((4 + ny + parts,)),
            dma((6,)),
            dma((6,)),
            dma((7,)),
            vm((1, FEAT), F32),
            vm((1, rows), jnp.int32),
            vm((1, rows), jnp.int32),
        ],
        name="heads_backward",
        compiler_params=pltpu.CompilerParams(
            collective_id=0, has_side_effects=True, vmem_limit_bytes=60 << 20
        ),
    )(hidden.T, res_bias, targets, loss_mask, res_weight[0].T, out_weight[0])
    return gh.T, gw.T[None], gb, loss.reshape(1)


def solution(mesh):
    placed = (
        P(None, "vocab"),
        P("head", None, "vocab"),
        P("head", "vocab"),
        P("head", "vocab", None),
        P("head", None),
        P("head", None),
    )
    return jax.shard_map(
        functools.partial(body, mesh.shape["head"], mesh.shape["vocab"]),
        mesh=mesh,
        in_specs=placed,
        out_specs=(P(None, "vocab"), P("head", None, "vocab"), P("head", "vocab"), P("head")),
        check_vma=False,
    )
```

```python
import functools

import jax
import jax.numpy as jnp
from jax import lax
from jax.experimental import pallas as pl
from jax.experimental.pallas import tpu as pltpu
from jax.sharding import PartitionSpec as P

MESH = pl.DeviceIdType.MESH
F32, BF16 = jnp.float32, jnp.bfloat16
GRID = {128: (4, 16), 16: (2, 4), 8: (2, 2)}
FEAT = 32
PARTS = 8


class Place:
    def __init__(self, heads, vocab):
        self.heads = heads
        self.ny, self.nz = GRID[vocab]
        v = lax.axis_index("vocab")
        self.x = lax.axis_index("head")
        self.v = v
        self.y = lax.div(v, 2 * self.nz)
        self.z = lax.rem(lax.div(v, 2), self.nz)
        self.c = lax.rem(v, 2)
        half = self.nz // 2
        self.dist = sorted(range(self.nz), key=lambda d: (-min(d, self.nz - d), d))
        self.slot_of = {d: j for j, d in enumerate(self.dist)}
        self.half = half
        self.parts = min(PARTS, self.nz)
        self.gs = self.nz // self.parts
        self.reach = self.nz // 4
        self.sib = (self.x, v + 1 - 2 * self.c)
        self.ydist = sorted(range(1, self.ny), key=lambda d: (-min(d, self.ny - d), d))

    def slot(self, z_abs):
        d = lax.rem(z_abs - self.z + self.nz, self.nz)
        return jnp.where(d >= self.half, jnp.where(d == self.half, 0, 2 * (d - self.half)), 2 * (self.half - d) - 1)

    def gather_slot(self, d):
        r = self.reach
        return jnp.where(
            d == 0,
            4 * r - 1,
            jnp.where(
                d <= r,
                3 * r - 2 + d,
                jnp.where(d < 2 * r, d - 1, jnp.where(d < 3 * r, 3 * r - 1 - d, 6 * r - 2 - d)),
            ),
        )

    def yat(self, d):
        return lax.rem(self.y + d + self.ny, self.ny)

    def zat(self, d):
        return lax.rem(self.z + d + self.nz, self.nz)

    def dev(self, y, z, c):
        return (self.x, (y * self.nz + z) * 2 + c)


def remote(src, dst, send, recv, dev):
    return pltpu.make_async_remote_copy(
        src_ref=src, dst_ref=dst, send_sem=send, recv_sem=recv, device_id=dev, device_id_type=MESH
    )


class Sends:
    def __init__(self, pt):
        self.pt = pt
        self.open = []

    def add(self, ref, sem):
        self.open.append((ref, sem))

    def flush(self):
        for ref, sem in self.open:
            remote(ref, ref, sem, sem, self.pt.sib).wait_send()
        self.open = []


def arrived(pt, ref, sem):
    remote(ref, ref, sem, sem, pt.sib).wait_recv()


def gather(pt, buf, sems, sends, between=None, late=None):
    zs, ys, cs, cr = (sems.at[k] for k in range(4))
    own = pt.nz - 1
    c = pt.c
    r = pt.reach
    behind, ahead = 2 * r - 1, 3 * r - 1
    groups = ((behind, pt.nz), (0, behind))
    for i in reversed(range(r)):
        for d, there, sem in ((i + 1, behind + i, 4), (-i - 1, ahead + i, 5)):
            remote(buf.at[c, 0, own], buf.at[c, 0, there], zs, sems.at[sem], pt.dev(pt.y, pt.zat(d), c)).start()
    if between is not None:
        between()
    for first, n, there, d, sem in ((behind, r, 0, r, 4), (ahead, r - 1, r, -r, 5)):
        arrived(pt, buf.at[c, 0, pl.ds(first, r)], sems.at[sem])
        if n:
            remote(
                buf.at[c, 0, pl.ds(first, n)],
                buf.at[c, 0, pl.ds(there, n)],
                zs,
                sems.at[6],
                pt.dev(pt.y, pt.zat(d), c),
            ).start()

    def across(rows, lo, hi):
        part = buf.at[c, pl.ds(*rows), pl.ds(lo, hi - lo)]
        remote(part, part, cs, cr, pt.sib).start()

    for g, (lo, hi) in enumerate(groups):
        if g == 1:
            arrived(pt, buf.at[c, 0, pl.ds(lo, hi - lo)], sems.at[6])
        for d in pt.ydist:
            remote(
                buf.at[c, 0, pl.ds(lo, hi - lo)],
                buf.at[c, d, pl.ds(lo, hi - lo)],
                ys,
                sems.at[7 + g],
                pt.dev(pt.yat(d), pt.z, c),
            ).start()
        across((0, 1), lo, hi)
    for g, (lo, hi) in enumerate(groups):
        arrived(pt, buf.at[c, pl.ds(1, pt.ny - 1), pl.ds(lo, hi - lo)], sems.at[7 + g])
        across((1, pt.ny - 1), lo, hi)
        if g == 0 and late is not None:
            late()
    arrived(pt, buf.at[1 - c], cr)
    sends.add(buf.at[c, 0, pl.ds(0, own)], zs)
    sends.add(buf.at[c, pl.ds(1, pt.ny - 1)], ys)
    sends.add(buf.at[c], cs)


def in_order(pt, buf, flat):
    def step(i, carry):
        y, z = lax.div(i, pt.nz), lax.rem(i, pt.nz)
        j = pt.gather_slot(lax.rem(z - pt.z + pt.nz, pt.nz))
        y = lax.rem(pt.y - y + pt.ny, pt.ny)
        for core in range(2):
            flat[pl.ds(pl.multiple_of((i * 2 + core) * FEAT, FEAT), FEAT), :] = buf[core, y, j]
        return carry

    lax.fori_loop(0, pt.ny * pt.nz, step, 0, unroll=4)


def send_along_z(pt, src, dst, j, send, recv):
    d = pt.dist[j]
    there = pt.slot_of[(pt.nz - d) % pt.nz]
    remote(
        src.at[pl.ds(j * FEAT, FEAT)], dst.at[there], send, recv, pt.dev(pt.y, pt.zat(d), pt.c)
    ).start()


def scatter(pt, term, own, bufs, sems, sends, ready=None, beside=None, late=None, combine=None):
    to_core, from_core, to_y, from_y, to_z, from_z = bufs
    cs, ys, zs, zr = (sems.at[k] for k in range(4))
    n = pt.gs * FEAT
    last = pt.parts - 1

    def rows(g):
        return pl.ds(g * n, n)

    for d in pt.ydist + [0]:
        to_core[d] = term(1 - pt.c, pt.yat(d)).astype(BF16)
        remote(to_core.at[d], from_core.at[d], cs, sems.at[4 + d], pt.sib).start()
    for d in pt.ydist + [0]:
        own[d] = term(pt.c, pt.yat(d))
    sends.flush()
    sends.add(to_core, cs)
    factors = ready() if ready is not None else None

    def both(d, g):
        mine, other = own[d, rows(g), :], from_core[d, rows(g), :].astype(F32)
        return mine + other if factors is None else factors[0] * mine + factors[1] * other

    for g in range(pt.parts):
        for d in pt.ydist:
            if g == 0:
                arrived(pt, from_core.at[d], sems.at[4 + d])
            to_y[d - 1, rows(g), :] = both(d, g).astype(BF16)
            remote(
                to_y.at[d - 1, rows(g)],
                from_y.at[d - 1, rows(g)],
                ys,
                sems.at[4 + pt.ny + g],
                pt.dev(pt.yat(d), pt.z, pt.c),
            ).start()
    sends.add(to_y, ys)
    arrived(pt, from_core.at[0], sems.at[4])
    if beside is not None:
        beside()
    for g in range(pt.parts):
        acc = both(0, g)
        arrived(pt, from_y.at[:, rows(g)], sems.at[4 + pt.ny + g])
        for d in pt.ydist:
            acc = acc + from_y[d - 1, rows(g), :].astype(F32)
        to_z[rows(g), :] = acc.astype(BF16)
        if g == last:
            total = acc[n - FEAT :, :]
        for j in range(g * pt.gs, min((g + 1) * pt.gs, pt.nz - 1)):
            send_along_z(pt, to_z, from_z, j, zs, zr)
    sends.flush()
    if late is not None:
        late()
    sends.add(to_z.at[pl.ds(0, (pt.nz - 1) * FEAT)], zs)
    arrived(pt, from_z.at[pl.ds(0, pt.nz - 1)], zr)
    others = [from_z[j].astype(F32) for j in range(pt.nz - 1)]
    return sum(others, total) if combine is None else combine(total, others)


def kernel(heads, vocab, *refs):
    (hid_hbm, bias_hbm, tgt_hbm, msk_hbm, wres_hbm, wout_hbm, gh_out, gw_out, gb_out, loss_out) = refs[:10]
    (wo, wot, wr, wrt, buf1, buf2, flat1, flat2, logits, eo, hits, own, gw, st, st_y, sz, st_z, gx, gx_in) = refs[10:29]
    rs1, rs2 = refs[29:35], refs[35:41]
    t_to_core, t_from_core, t_mine, t_to_y, t_from_y, t_to_z, t_from_z = refs[41:48]
    ag1_s, ag2_s, rs1_s, rs2_s, t_s, tail_s, local = refs[48:55]
    bias, tgt, msk = refs[55:58]
    pt = Place(heads, vocab)
    ny, nz = pt.ny, pt.nz
    nrow = buf1.shape[-1]
    nvoc = wo.shape[0]
    feats = wo.shape[1]
    ychunk = feats // ny
    sends = Sends(pt)

    hid = buf1.at[pt.c, 0, nz - 1]
    get_wr = pltpu.make_async_copy(wres_hbm, wr, local.at[0])
    get_wo = pltpu.make_async_copy(wout_hbm, wo, local.at[1])
    get_hid = pltpu.make_async_copy(hid_hbm, hid, local.at[3])
    get_small = [
        pltpu.make_async_copy(src, dst, local.at[4 + k])
        for k, (src, dst) in enumerate(((bias_hbm, bias), (tgt_hbm, tgt), (msk_hbm, msk)))
    ]
    for cp in [get_hid, get_wr, *get_small, get_wo]:
        cp.start()

    peers = [pt.dev(pt.y, pt.zat(d), pt.c) for k in range(pt.reach, 0, -1) for d in (k, -k)]
    plane = [(dy, dc) for dy in range(ny) for dc in range(2) if dy or dc]
    near = [pt.dev(pt.yat(dy), pt.z, lax.rem(pt.c + dc, 2)) for dy, dc in plane]
    xpeers = [(lax.rem(pt.x + d, heads), pt.v) for d in range(1, heads)]
    barrier = pltpu.get_barrier_semaphore()
    for dev in peers + near + xpeers:
        pl.semaphore_signal(barrier, inc=1, device_id=dev, device_id_type=MESH)

    per = 256 // (2 * FEAT)

    def place_rows(dst, chunk, i):
        y = lax.div(i * per, nz)
        z0 = lax.rem(i * per, nz)
        for k in range(per):
            j = pt.slot(z0 + k)
            for core in range(2):
                r = (k * 2 + core) * FEAT
                dst[core, y, j] = chunk[r : r + FEAT, :]

    def turn_wr(i, carry):
        place_rows(wrt, wr[:, pl.ds(pl.multiple_of(i * 256, 256), 256)].T, i)
        return carry

    for cp in get_small:
        cp.wait()
    get_hid.wait()
    pl.semaphore_wait(barrier, len(peers) + len(near) + len(xpeers))

    def turn_wo(i, carry):
        place_rows(wot, wo[:, pl.ds(pl.multiple_of(i * 256, 256), 256)].T, i)
        return carry

    def turn():
        get_wr.wait()
        lax.fori_loop(0, feats // 256, turn_wr, 0)
        get_wo.wait()
        lax.fori_loop(0, feats // 256, turn_wo, 0)

    ids = pt.v * nvoc + lax.broadcasted_iota(jnp.int32, (nvoc, nrow), 0)

    def rows_of(core, y):
        w = wot[core, y].reshape(nz * FEAT, nvoc)
        return jnp.dot(w, hits[...], preferred_element_type=F32).astype(BF16)

    def prepare():
        hits[...] = (ids == tgt[...]).astype(BF16)
        for d in range(ny):
            t_to_core[d] = rows_of(1 - pt.c, pt.yat(d))
        remote(t_to_core, t_from_core, t_s.at[0], t_s.at[1], pt.sib).start()
        sends.add(t_to_core, t_s.at[0])
        for d in range(ny):
            t_mine[d] = rows_of(pt.c, pt.yat(d))

    gather(pt, buf1, ag1_s, sends, turn, prepare)
    in_order(pt, buf1, flat1)

    eye = lax.broadcasted_iota(jnp.int32, (FEAT, FEAT), 0) == lax.broadcasted_iota(jnp.int32, (FEAT, FEAT), 1)
    bias_col = jnp.sum(jnp.where(eye, bias[...], 0.0), axis=1, keepdims=True)
    pre = jnp.zeros((FEAT, nrow), F32)
    for y in range(ny):
        pre = pre + jnp.dot(
            wr[:, y * ychunk : (y + 1) * ychunk], flat1[y * ychunk : (y + 1) * ychunk, :], preferred_element_type=F32
        )
    pre = pre + bias_col
    sig = jax.nn.sigmoid(pre)
    buf2[pt.c, 0, nz - 1] = (hid[...].astype(F32) + pre * sig).astype(BF16)
    gate = sig * (1.0 + pre * (1.0 - sig))


    def target_rows():
        arrived(pt, t_from_core, t_s.at[1])
        for d in pt.ydist:
            t_to_y[d - 1] = t_mine[d] + t_from_core[d]
            remote(t_to_y.at[d - 1], t_from_y.at[d - 1], t_s.at[2], t_s.at[3], pt.dev(pt.yat(d), pt.z, pt.c)).start()
        sends.flush()
        sends.add(t_to_y, t_s.at[2])

    def target_rows_z():
        arrived(pt, t_from_y, t_s.at[3])
        rows = t_mine[0] + t_from_core[0]
        for d in pt.ydist:
            rows = rows + t_from_y[d - 1]
        t_to_z[...] = rows
        for j in range(nz - 1):
            send_along_z(pt, t_to_z, t_from_z, j, t_s.at[4], t_s.at[5])
        sends.add(t_to_z.at[pl.ds(0, (nz - 1) * FEAT)], t_s.at[4])

    gather(pt, buf2, ag2_s, sends, target_rows, target_rows_z)
    in_order(pt, buf2, flat2)

    logits[...] = jnp.zeros_like(logits)

    def logit_step(i, carry):
        at = pl.ds(pl.multiple_of(i * ychunk, ychunk), ychunk)
        logits[...] += jnp.dot(wo[:, at], flat2[at, :], preferred_element_type=F32)
        return carry

    lax.fori_loop(0, ny, logit_step, 0)
    hit = ids == tgt[...]
    lg = logits[...]
    top = jnp.max(lg, axis=0, keepdims=True)
    picked = jnp.sum(jnp.where(hit, lg, 0.0), axis=0, keepdims=True)
    e = jnp.exp(lg - top)
    e_hit = jnp.sum(jnp.where(hit, e, 0.0), axis=0, keepdims=True)
    e = jnp.where(hit, 0.0, e)
    rest = jnp.sum(e, axis=0, keepdims=True)
    eo[...] = e.astype(BF16)

    def pack(*values):
        r = lax.broadcasted_iota(jnp.int32, (8, nrow), 0)
        out = jnp.zeros((8, nrow), F32)
        for k, value in enumerate(values):
            out = jnp.where(r == k, value, out)
        return out

    def merge(ref, count):
        tops = [ref[i, 0:1, :] for i in range(count)]
        best = functools.reduce(jnp.maximum, tops)
        scale = [jnp.exp(t - best) for t in tops]
        others = sum(ref[i, 1:2, :] * scale[i] for i in range(count))
        target = sum(ref[i, 2:3, :] * scale[i] for i in range(count))
        pick = sum(ref[i, 3:4, :] for i in range(count))
        return best, others, target, pick

    packed = pack(top, rest, e_hit, picked)
    st[...] = packed
    me = pt.y * 2 + pt.c
    st_y[me] = packed
    for dev in near:
        remote(st, st_y.at[me], tail_s.at[0], tail_s.at[1], dev).start()

    plane_stats = []

    def stats_near():
        arrived(pt, st_y.at[pl.ds(0, 2 * ny - 1)], tail_s.at[1])
        sends.add(st_y.at[pl.ds(0, 2 * ny - 1)], tail_s.at[0])
        plane_stats.extend(merge(st_y, 2 * ny))
        return jnp.exp(top - plane_stats[0]), jnp.exp(st_y[me + 1 - 2 * pt.c, 0:1, :] - plane_stats[0])

    def stats_out():
        packed = pack(*plane_stats)
        sz[...] = packed
        st_z[pt.z] = packed
        for d in pt.dist[:-1]:
            remote(sz, st_z.at[pt.z], tail_s.at[2], tail_s.at[3], pt.dev(pt.y, pt.zat(d), pt.c)).start()

    def weigh(mine, others):
        arrived(pt, st_z.at[pl.ds(0, nz - 1)], tail_s.at[3])
        sends.add(st_z.at[pl.ds(0, nz - 1)], tail_s.at[2])
        best, rest, target, pick = merge(st_z, nz)
        total = rest + target
        lse = best + jnp.log(total)
        factor = jnp.float32(0.8**heads)
        for k in range(heads - 1):
            factor = jnp.where(pt.x == k, jnp.float32(0.8 ** (k + 1)), factor)
        weight = factor * msk[...].astype(F32) / nrow
        loss_out[...] = jnp.sum(weight * (lse - pick), axis=1, keepdims=True)
        beta = (-weight * (rest / total)).astype(BF16).astype(F32)
        arrived(pt, t_from_z.at[pl.ds(0, nz - 1)], t_s.at[5])
        rows = t_to_z[(nz - 1) * FEAT :, :].astype(F32)
        out = jnp.exp(plane_stats[0] - lse) * mine
        for j in range(nz - 1):
            rows = rows + t_from_z[j].astype(F32)
            out = out + jnp.exp(st_z[pt.zat(pt.dist[j]), 0:1, :] - lse) * others[j]
        return weight * out + beta * rows

    def vocab_term(core, y):
        return jnp.dot(wot[core, y].reshape(nz * FEAT, nvoc), eo[...], preferred_element_type=F32)

    dh = scatter(pt, vocab_term, own, rs1, rs1_s, sends, stats_near, stats_out, None, weigh)
    dpre = (dh * gate).astype(BF16)
    gb = jnp.sum(dpre.astype(F32), axis=1, keepdims=True)
    gb_out[...] = jnp.sum(jnp.where(eye, gb, 0.0), axis=0, keepdims=True)

    put_gw = pltpu.make_async_copy(gw, gw_out, local.at[2])

    def weight_grad():
        def step(i, carry):
            at = pl.ds(pl.multiple_of(i * 256, 256), 256)
            gw[:, at] = lax.dot_general(
                dpre, flat1[at, :], (((1,), (1,)), ((), ())), preferred_element_type=F32
            )
            return carry

        lax.fori_loop(0, feats // 256, step, 0)
        put_gw.start()

    def residual_term(core, y):
        return jnp.dot(wrt[core, y].reshape(nz * FEAT, FEAT), dpre, preferred_element_type=F32)

    back = scatter(pt, residual_term, own, rs2, rs2_s, sends, late=weight_grad)
    part = dh + back
    gx[...] = part
    gx_in[pt.x] = part
    for dev in xpeers:
        remote(gx, gx_in.at[pt.x], tail_s.at[4], tail_s.at[5], dev).start()
    sends.flush()
    put_gw.wait()
    if heads > 1:
        others = gx_in.at[pl.ds(0, heads - 1)]
        arrived(pt, others, tail_s.at[5])
        sends.add(others, tail_s.at[4])
    gh_out[...] = sum(gx_in[k] for k in range(heads))
    sends.flush()


def body(heads, vocab, hidden, res_weight, res_bias, out_weight, targets, loss_mask):
    ny, nz = GRID[vocab]
    rows = hidden.shape[0]
    nvoc, feats = out_weight.shape[1:]
    parts = min(PARTS, nz)
    dma = pltpu.SemaphoreType.DMA
    vm = pltpu.VMEM
    scatter_bufs = [
        vm((ny, nz * FEAT, rows), BF16),
        vm((ny, nz * FEAT, rows), BF16),
        vm((ny - 1, nz * FEAT, rows), BF16),
        vm((ny - 1, nz * FEAT, rows), BF16),
        vm((nz * FEAT, rows), BF16),
        vm((nz, FEAT, rows), BF16),
    ]
    in_vmem = pl.BlockSpec(memory_space=pltpu.VMEM)
    anywhere = pl.BlockSpec(memory_space=pl.ANY)
    gh, gw, gb, loss = pl.pallas_call(
        functools.partial(kernel, heads, vocab),
        out_shape=(
            vm((FEAT, rows), F32),
            vm((FEAT, feats), F32),
            vm((1, FEAT), F32),
            jax.ShapeDtypeStruct((1, 1), F32),
        ),
        in_specs=[anywhere] * 6,
        out_specs=(in_vmem, in_vmem, in_vmem, in_vmem),
        scratch_shapes=[
            vm((nvoc, feats), BF16),
            vm((2, ny, nz, FEAT, nvoc), BF16),
            vm((FEAT, feats), BF16),
            vm((2, ny, nz, FEAT, FEAT), BF16),
            vm((2, ny, nz, FEAT, rows), BF16),
            vm((2, ny, nz, FEAT, rows), BF16),
            vm((feats, rows), BF16),
            vm((feats, rows), BF16),
            vm((nvoc, rows), F32),
            vm((nvoc, rows), BF16),
            vm((nvoc, rows), BF16),
            vm((ny, nz * FEAT, rows), F32),
            vm((FEAT, feats), F32),
            vm((8, rows), F32),
            vm((2 * ny, 8, rows), F32),
            vm((8, rows), F32),
            vm((nz, 8, rows), F32),
            vm((FEAT, rows), F32),
            vm((heads, FEAT, rows), F32),
            *scatter_bufs,
            *scatter_bufs,
            vm((ny, nz * FEAT, rows), BF16),
            vm((ny, nz * FEAT, rows), BF16),
            vm((ny, nz * FEAT, rows), BF16),
            vm((ny - 1, nz * FEAT, rows), BF16),
            vm((ny - 1, nz * FEAT, rows), BF16),
            vm((nz * FEAT, rows), BF16),
            vm((nz, FEAT, rows), BF16),
            dma((9,)),
            dma((9,)),
            dma((4 + ny + parts,)),
            dma((4 + ny + parts,)),
            dma((6,)),
            dma((6,)),
            dma((7,)),
            vm((1, FEAT), F32),
            vm((1, rows), jnp.int32),
            vm((1, rows), jnp.int32),
        ],
        name="heads_backward",
        compiler_params=pltpu.CompilerParams(
            collective_id=0, has_side_effects=True, vmem_limit_bytes=60 << 20
        ),
    )(hidden.T, res_bias, targets, loss_mask, res_weight[0].T, out_weight[0])
    return gh.T, gw.T[None], gb, loss.reshape(1)


def solution(mesh):
    placed = (
        P(None, "vocab"),
        P("head", None, "vocab"),
        P("head", "vocab"),
        P("head", "vocab", None),
        P("head", None),
        P("head", None),
    )
    return jax.shard_map(
        functools.partial(body, mesh.shape["head"], mesh.shape["vocab"]),
        mesh=mesh,
        in_specs=placed,
        out_specs=(P(None, "vocab"), P("head", None, "vocab"), P("head", "vocab"), P("head")),
        check_vma=False,
    )
```
